32 devices in a mesh: grp: 4 (over z), ep: 8 (over y, x, core).
Axes of the slice: x: 2, y: 2, z: 4, core: 2. Of those that a mesh axis runs over, the one named last changes fastest.
Arguments:
- tokens: bfloat16 [4096, 2048], P(('grp', 'ep')), may hold values from -6 to 6
- out_grad: bfloat16 [4096, 2048], P(('grp', 'ep')), may hold values from -1.5 to 1.5
- routes: int32 [4096, 2], P(('grp', 'ep')), may hold values from 0 to 3, as said below
- gates: bfloat16 [4096, 2], P(('grp', 'ep')), may hold values from 0.099609375 to 1
- w_gate_up: bfloat16 [8, 2048, 1024], P('ep', 'grp'), may hold values from -0.125 to 0.125
- w_down: bfloat16 [8, 2048, 512], P('ep', 'grp'), may hold values from -0.25 to 0.25
- plan: int32 [8], replicated, may hold values from 0 to 3, as said below
- failed: int32 [4, 8], replicated, may hold values from 0 to 1, as said below
Outputs:
- token_grad: bfloat16 [4096, 2048], P(('grp', 'ep'))
- gate_grad: bfloat16 [4096, 2], P(('grp', 'ep'))
- weight_grad: float32 [4, 2048, 1536], P(None, ('grp', 'ep'))
The draws below stay inside these ranges and needn't reach their ends.
Inputs may be any that keep to these rules, and one draw needn't show every extreme that they name: `plan`: each expert is hosted by one or three slots. Each group has one to 1 failed slots, and every expert keeps a live replica in every group. A token names 2 different experts. Under the replica rule the routes of one device reach any slot at most 40 times, and in every group some slot receives exactly 40 routes from every device of the group.
All inputs are finite; a program needn't handle non-finite values.
Results may differ from the reference program's by a relative error of at most 0.0058.
Values may be sent and summed in bfloat16 or wider, within the bound.
A program may use at most 128 MiB of HBM per device.

```python
import math
from functools import partial
import jax
import jax.numpy as jnp
from jax import lax

D = 2048
FF = 512
TOPK = 2
TOK_DEV = 128
EXPERTS = 4
CAP = 40
MAXFAIL = 1
TOKENS = 4096
N_GRP = 4
N_EP = 8


def layout(key):
    base_key = jax.random.fold_in(key, 4111)
    slot_order = jax.random.permutation(jax.random.fold_in(base_key, 1), N_EP)
    expert_order = jax.random.permutation(jax.random.fold_in(base_key, 2), EXPERTS)
    position = jnp.arange(N_EP)
    extra_rank = jnp.maximum(position - EXPERTS, 0)
    owners = jnp.where(position < EXPERTS, expert_order[position % EXPERTS], expert_order[extra_rank // 2])
    plan = jnp.zeros((N_EP,), jnp.int32).at[slot_order].set(owners.astype(jnp.int32))

    def group_failures(group_index):
        group_key = jax.random.fold_in(jax.random.fold_in(base_key, 3), group_index)
        fail_count = jax.random.randint(jax.random.fold_in(group_key, 1), (), 1, MAXFAIL + 1)
        extra_order = jax.random.permutation(jax.random.fold_in(group_key, 2), EXPERTS)
        dead_slots = jnp.concatenate([jnp.zeros((EXPERTS,), jnp.int32), (extra_order < fail_count).astype(jnp.int32)])
        return jnp.zeros((N_EP,), jnp.int32).at[slot_order].set(dead_slots)
    failed = jax.vmap(group_failures)(jnp.arange(N_GRP))
    full_expert = jax.random.randint(jax.random.fold_in(base_key, 4), (N_GRP,), 0, EXPERTS)
    return (plan, failed.astype(jnp.int32), full_expert)


def draw_plan(key, part):
    return layout(key)[0]


def draw_failed(key, part):
    return layout(key)[1]


def device_table(key, plan, failed, full_expert, group_index, device_index):
    entry_slot = jnp.arange(N_EP * CAP) // CAP
    entry_expert = plan[entry_slot]
    device_key = jax.random.fold_in(jax.random.fold_in(key, 5333), group_index * N_EP + device_index)
    usable = 1 - failed[group_index][entry_slot]
    priority = jnp.where(entry_expert == full_expert[group_index], 2, 1) * usable
    noise = jax.random.randint(jax.random.fold_in(device_key, 1), (N_EP * CAP,), 0, 16384)
    scores = priority * 134217728 + noise * 4096 + jnp.arange(N_EP * CAP)
    chosen = entry_expert[jnp.argsort(-scores)[:TOK_DEV * TOPK]]
    table = jnp.sort(chosen).reshape(TOPK, TOK_DEV).T
    flips = jax.random.randint(jax.random.fold_in(device_key, 2), (TOK_DEV, 1), 0, 2)
    table = jnp.where(flips == 1, table[:, ::-1], table)
    token_order = jax.random.permutation(jax.random.fold_in(device_key, 3), TOK_DEV)
    return table[token_order]


def draw_routes(key, part):
    plan, failed, full_expert = layout(key)

    def per_group(group_index):
        return jax.vmap(partial(device_table, key, plan, failed, full_expert, group_index))(jnp.arange(N_EP))
    grid = jax.vmap(per_group)(jnp.arange(N_GRP))
    return grid.reshape(TOKENS, TOPK).astype(jnp.int32)


def levels(stream_key, shape, cuts, smallest, top_value):
    gain = 1.0
    for dim, blocks in cuts:
        draws = jax.random.uniform(jax.random.fold_in(jax.random.fold_in(stream_key, 6), dim), (blocks,), jnp.float32, smallest / len(cuts), top_value / len(cuts))
        gain = gain * jnp.repeat(jnp.exp(draws), shape[dim] // blocks).reshape((-1,) + (1,) * (len(shape) - 1 - dim))
    return gain


def normal_values(key, extent, scale, reach, pieces=(), kind=jnp.bfloat16):
    values = jax.random.normal(key, extent, jnp.float32) * scale
    if len(pieces) > 0:
        values = levels(key, extent, pieces, -0.22, 0.18) * values
    return jnp.clip(values, min=-reach, max=reach).astype(kind)


def setup_inputs(seed: int = 0) -> dict:
    key_of = jax.random.split(jax.random.key(seed), 9)
    tokens = normal_values(key_of[0], (TOKENS, D), 1.0, 6.0, ((0, 32),))
    out_grad = normal_values(key_of[1], (TOKENS, D), 0.25, 1.5, ((0, 32),))
    routes = draw_routes(jax.random.fold_in(key_of[8], 71), 0)
    gates = jnp.clip(jnp.exp(math.log(1.0) - 2.306499 * jax.random.uniform(key_of[3], (TOKENS, TOPK), jnp.float32) ** levels(key_of[3], (TOKENS, TOPK), ((0, 32),), -0.2, 0.2)), 0.099609375, 1.0).astype(jnp.bfloat16)
    w_gate_up = normal_values(key_of[4], (N_EP, D, 2 * FF), D ** -0.5, 0.125, ((0, 8), (1, 4)))
    w_down = normal_values(key_of[5], (N_EP, D, FF), FF ** -0.5, 0.25, ((0, 8), (1, 4)))
    plan = draw_plan(jax.random.fold_in(key_of[8], 71), 0)
    failed = draw_failed(jax.random.fold_in(key_of[8], 71), 0)
    return dict(tokens=tokens, out_grad=out_grad, routes=routes, gates=gates, w_gate_up=w_gate_up, w_down=w_down, plan=plan, failed=failed)


def assign(route_ids, hosting, in_service, capacity, experts):
    route_count = route_ids.shape[0] * route_ids.shape[1]
    slot_count = hosting.shape[0]
    flat_routes = route_ids.reshape(route_count)
    expert_ids = jnp.arange(experts, dtype=jnp.int32)
    hosted = ((hosting[None, :] == expert_ids[:, None]) & (in_service[None, :] > 0)).astype(jnp.int32)
    replicas = jnp.sum(hosted, axis=1)
    ordinal = jnp.sum(hosted * (jnp.cumsum(hosted, axis=1) - 1), axis=0)
    expert_hot = (flat_routes[:, None] == expert_ids[None, :]).astype(jnp.int32)
    expert_rank = jnp.sum(expert_hot * (jnp.cumsum(expert_hot, axis=0) - 1), axis=1)
    route_replicas = jnp.sum(expert_hot * replicas[None, :], axis=1)
    replica_pick = expert_rank % route_replicas
    slot_hot = ((hosting[None, :] == flat_routes[:, None]) & (in_service[None, :] > 0)
                & (ordinal[None, :] == replica_pick[:, None])).astype(jnp.int32)
    slot_rank = jnp.sum(slot_hot * (jnp.cumsum(slot_hot, axis=0) - 1), axis=1)
    slot_index = jnp.sum(slot_hot * jnp.arange(slot_count, dtype=jnp.int32)[None, :], axis=1)
    return (slot_index * capacity + slot_rank).astype(jnp.int32)


def expert_rows(rows_x, rows_dy, rows_gate, full_gu, full_dn):
    hidden_width = full_dn.shape[1]
    projected = jnp.dot(rows_x, full_gu, preferred_element_type=jnp.float32)
    gate_pre = projected[:, :hidden_width]
    up_pre = projected[:, hidden_width:]
    sigmoid_a = jax.nn.sigmoid(gate_pre)
    silu_a = gate_pre * sigmoid_a
    hidden = (silu_a * up_pre).astype(jnp.bfloat16)
    upstream = jnp.dot(rows_dy, full_dn, preferred_element_type=jnp.float32)
    rebuilt = jnp.dot(hidden, full_dn.T, preferred_element_type=jnp.float32)
    gate_grad = jnp.sum(rows_dy.astype(jnp.float32) * rebuilt, axis=1).astype(jnp.bfloat16)
    gate_value = rows_gate.astype(jnp.float32)[:, None]
    hidden_grad = gate_value * upstream
    gate_delta = hidden_grad * up_pre * sigmoid_a * (1.0 + gate_pre * (1.0 - sigmoid_a))
    up_delta = hidden_grad * silu_a
    pre_grad = jnp.concatenate([gate_delta, up_delta], axis=1).astype(jnp.bfloat16)
    row_grad = jnp.dot(pre_grad, full_gu.T, preferred_element_type=jnp.float32).astype(jnp.bfloat16)
    gated_hidden = (gate_value * hidden.astype(jnp.float32)).astype(jnp.bfloat16)
    grad_gu = jnp.dot(rows_x.T, pre_grad, preferred_element_type=jnp.float32)
    grad_dn = jnp.dot(rows_dy.T, gated_hidden, preferred_element_type=jnp.float32)
    return row_grad, gate_grad, grad_gu, grad_dn


def reference(tokens, out_grad, routes, gates, w_gate_up, w_down, plan, failed):
    route_count = TOK_DEV * TOPK
    buffer_rows = N_EP * CAP
    expert_ids = jnp.arange(EXPERTS, dtype=jnp.int32)
    token_groups = tokens.reshape(N_GRP, N_EP, TOK_DEV, D)
    grad_groups = out_grad.reshape(N_GRP, N_EP, TOK_DEV, D)
    route_groups = routes.reshape(N_GRP, N_EP, TOK_DEV, TOPK)
    gate_groups = gates.reshape(N_GRP, N_EP, TOK_DEV, TOPK)

    def to_slots(array):
        shaped = array.reshape((N_EP, N_EP, CAP) + array.shape[2:])
        shaped = jnp.swapaxes(shaped, 0, 1)
        return shaped.reshape((N_EP, N_EP * CAP) + array.shape[2:])

    def group_step(running, inputs):
        group_tokens, group_grads, group_routes, group_gates, group_failed = inputs
        in_service = 1 - group_failed
        positions = jax.vmap(lambda route_ids: assign(route_ids, plan, in_service, CAP, EXPERTS))(group_routes)

        def pack(slot_pos, dev_tokens, dev_grads, dev_gates):
            source = jnp.full((buffer_rows,), route_count, jnp.int32).at[slot_pos].set(
                jnp.arange(route_count, dtype=jnp.int32))
            token_of = (source // TOPK).astype(jnp.int32)
            zero_row = jnp.zeros((1, D), jnp.bfloat16)
            rows_x = jnp.concatenate([dev_tokens, zero_row], axis=0)[token_of]
            rows_dy = jnp.concatenate([dev_grads, zero_row], axis=0)[token_of]
            rows_gate = jnp.concatenate([dev_gates.reshape(route_count), jnp.zeros((1,), jnp.bfloat16)])[source]
            return rows_x, rows_dy, rows_gate

        packed_x, packed_dy, packed_gate = jax.vmap(pack)(positions, group_tokens, group_grads, group_gates)

        def per_slot(operands):
            return expert_rows(*operands)

        row_grads, gate_rows, grad_gu, grad_dn = lax.map(
            per_slot, (to_slots(packed_x), to_slots(packed_dy), to_slots(packed_gate), w_gate_up, w_down))
        slot_grad = jnp.concatenate([grad_gu, grad_dn], axis=2).astype(jnp.bfloat16)
        hosted = ((plan[None, :] == expert_ids[:, None]) & (in_service[None, :] > 0)).astype(jnp.float32)
        group_grad = jnp.einsum("es,sdc->edc", hosted, slot_grad.astype(jnp.float32))
        running = running + group_grad
        back_x = to_slots(row_grads)
        back_gate = to_slots(gate_rows)

        def unpack(slot_pos, dev_back_x, dev_back_gate):
            gathered = dev_back_x[slot_pos].reshape(TOK_DEV, TOPK, D).astype(jnp.float32)
            summed = jnp.sum(gathered, axis=1).astype(jnp.bfloat16)
            return summed, dev_back_gate[slot_pos].reshape(TOK_DEV, TOPK)

        group_dx, group_dg = jax.vmap(unpack)(positions, back_x, back_gate)
        return running, (group_dx, group_dg)

    initial = jnp.zeros((EXPERTS, D, 3 * FF), jnp.float32)
    final, outputs = lax.scan(group_step, initial,
                              (token_groups, grad_groups, route_groups, gate_groups, failed))
    token_grad = outputs[0].reshape(TOKENS, D)
    gate_grad = outputs[1].reshape(TOKENS, TOPK)
    return token_grad, gate_grad, final / N_GRP
```

```python
import functools

import jax
import jax.numpy as jnp
from jax import lax
from jax.experimental import pallas as pl
from jax.experimental.pallas import tpu as pltpu
from jax.sharding import PartitionSpec as P


def assign(route_ids, hosting, in_service, capacity, experts):
    route_count = route_ids.shape[0] * route_ids.shape[1]
    slot_count = hosting.shape[0]
    flat_routes = route_ids.reshape(route_count)
    expert_ids = jnp.arange(experts, dtype=jnp.int32)
    hosted = ((hosting[None, :] == expert_ids[:, None]) & (in_service[None, :] > 0)).astype(
        jnp.int32
    )
    replicas = jnp.sum(hosted, axis=1)
    ordinal = jnp.sum(hosted * (jnp.cumsum(hosted, axis=1) - 1), axis=0)
    expert_hot = (flat_routes[:, None] == expert_ids[None, :]).astype(jnp.int32)
    expert_rank = jnp.sum(expert_hot * (jnp.cumsum(expert_hot, axis=0) - 1), axis=1)
    route_replicas = jnp.sum(expert_hot * replicas[None, :], axis=1)
    replica_pick = expert_rank % route_replicas
    slot_hot = (
        (hosting[None, :] == flat_routes[:, None])
        & (in_service[None, :] > 0)
        & (ordinal[None, :] == replica_pick[:, None])
    ).astype(jnp.int32)
    slot_rank = jnp.sum(slot_hot * (jnp.cumsum(slot_hot, axis=0) - 1), axis=1)
    slot_index = jnp.sum(slot_hot * jnp.arange(slot_count, dtype=jnp.int32)[None, :], axis=1)
    return slot_index, slot_rank


def expert_rows(rows_x, rows_dy, rows_gate, full_gu, full_dn):
    hidden_width = full_dn.shape[1]
    projected = jnp.dot(rows_x, full_gu, preferred_element_type=jnp.float32)
    gate_pre = projected[:, :hidden_width]
    up_pre = projected[:, hidden_width:]
    sigmoid_a = jax.nn.sigmoid(gate_pre)
    silu_a = gate_pre * sigmoid_a
    hidden = (silu_a * up_pre).astype(jnp.bfloat16)
    upstream = jnp.dot(rows_dy, full_dn, preferred_element_type=jnp.float32)
    rebuilt = lax.dot_general(
        hidden, full_dn, (((1,), (1,)), ((), ())), preferred_element_type=jnp.float32
    )
    gate_grad = jnp.sum(rows_dy.astype(jnp.float32) * rebuilt, axis=1).astype(jnp.bfloat16)
    gate_value = rows_gate.astype(jnp.float32)[:, None]
    hidden_grad = gate_value * upstream
    gate_delta = hidden_grad * up_pre * sigmoid_a * (1.0 + gate_pre * (1.0 - sigmoid_a))
    up_delta = hidden_grad * silu_a
    pre_grad = jnp.concatenate([gate_delta, up_delta], axis=1).astype(jnp.bfloat16)
    row_grad = lax.dot_general(
        pre_grad, full_gu, (((1,), (1,)), ((), ())), preferred_element_type=jnp.float32
    ).astype(jnp.bfloat16)
    gated_hidden = (gate_value * hidden.astype(jnp.float32)).astype(jnp.bfloat16)
    grad_gu = lax.dot_general(
        rows_x, pre_grad, (((0,), (0,)), ((), ())), preferred_element_type=jnp.float32
    )
    grad_dn = lax.dot_general(
        rows_dy, gated_hidden, (((0,), (0,)), ((), ())), preferred_element_type=jnp.float32
    )
    return (row_grad, gate_grad, grad_gu, grad_dn)


MESH = pl.DeviceIdType.MESH
LANES = 128
ROW_TILE = 16


def fused_kernel(
    nz, ne, block,
    tok_ref, dy_ref, pack_ref, unpack_ref, gate_ref, gu_ref, dn_ref, mask_ref,
    tgrad_ref, ggrad_ref, wgrad_ref,
    weights, send_rows, rows, x_t, dy_t, row_acc, gate_acc, slot_grads, peer_grads,
    plane_sums, far_sums, ret, back,
    ag_send, ag_recv, out_send, out_recv, grad_send, grad_recv, sum_send, sum_recv,
    ret_send, ret_recv,
):
    z = lax.axis_index("grp")
    me = lax.axis_index("ep")
    chunks, _, shard, width3 = weights.shape
    model = nz * shard
    width = width3 // 3
    hidden_width = chunks * width
    experts = wgrad_ref.shape[0]
    own_rows = wgrad_ref.shape[1]
    count = ne * block
    f32, bf16 = jnp.float32, jnp.bfloat16

    barrier = pltpu.get_barrier_semaphore()
    for k in range(1, ne):
        pl.semaphore_signal(
            barrier, inc=1, device_id={"ep": lax.rem(me + k, ne)}, device_id_type=MESH
        )
    for k in range(1, nz):
        pl.semaphore_signal(
            barrier, inc=1, device_id={"grp": lax.rem(z + k, nz)}, device_id_type=MESH
        )

    for f in range(chunks):
        cols = slice(f * width, (f + 1) * width)
        weights[f, z, :, 0:width] = gu_ref[0, :, cols]
        weights[f, z, :, width : 2 * width] = gu_ref[
            0, :, hidden_width + f * width : hidden_width + (f + 1) * width
        ]
        weights[f, z, :, 2 * width : 3 * width] = dn_ref[0, :, cols]
    pl.semaphore_wait(barrier, ne - 1 + nz - 1)

    def shard_copy(f, owner, up):
        step = 1 if up else nz - 1
        return pltpu.make_async_remote_copy(
            src_ref=weights.at[f, owner],
            dst_ref=weights.at[f, owner],
            send_sem=ag_send.at[f, owner, 0 if up else 1],
            recv_sem=ag_recv.at[f, owner],
            device_id={"grp": lax.rem(z + step, nz)},
            device_id_type=MESH,
        )

    def start_own(f):
        @pl.when(z < nz - 1)
        def _():
            shard_copy(f, z, True).start()

        @pl.when(z > 0)
        def _():
            shard_copy(f, z, False).start()

    def arrive(f, hop):
        @pl.when(z >= hop)
        def _():
            shard_copy(f, z - hop, True).wait_recv()

            @pl.when(z < nz - 1)
            def _():
                shard_copy(f, z - hop, True).start()

        @pl.when(z + hop < nz)
        def _():
            shard_copy(f, z + hop, False).wait_recv()

            @pl.when(z > 0)
            def _():
                shard_copy(f, z + hop, False).start()

    def shard_sends_done():
        for f in range(chunks):
            for hop in range(nz):
                @pl.when((z >= hop) & (z < nz - 1))
                def _():
                    shard_copy(f, z - hop, True).wait_send()

                @pl.when((z + hop < nz) & (z > 0))
                def _():
                    shard_copy(f, z + hop, False).wait_send()

    def block_rows(k):
        return pl.ds(pl.multiple_of(k * block, ROW_TILE), block)

    def out_copy(k):
        return pltpu.make_async_remote_copy(
            src_ref=send_rows.at[block_rows(k)],
            dst_ref=rows.at[block_rows(k)],
            send_sem=out_send.at[k],
            recv_sem=out_recv.at[k],
            device_id={"ep": lax.rem(me + k, ne)},
            device_id_type=MESH,
        )

    def pack(k, target):
        here = block_rows(k)
        first, second = pack_ref[0, here, :], pack_ref[1, here, :]
        both = first + second
        target[here, 0:model] = jnp.dot(
            both, tok_ref[...], preferred_element_type=f32
        ).astype(bf16)
        target[here, model : 2 * model] = jnp.dot(
            both, dy_ref[...], preferred_element_type=f32
        ).astype(bf16)
        target[here, 2 * model : 2 * model + LANES] = (
            jnp.dot(first, gate_ref[0], preferred_element_type=f32)
            + jnp.dot(second, gate_ref[1], preferred_element_type=f32)
        ).astype(bf16)

    def grad_copy(f, k):
        return pltpu.make_async_remote_copy(
            src_ref=slot_grads.at[f, lax.rem(me + k, ne)],
            dst_ref=peer_grads.at[f, k],
            send_sem=grad_send.at[f, k],
            recv_sem=grad_recv.at[f, k],
            device_id={"ep": lax.rem(me + k, ne)},
            device_id_type=MESH,
        )

    def sum_copy(f, k):
        return pltpu.make_async_remote_copy(
            src_ref=plane_sums.at[f, lax.rem(z + k, nz)],
            dst_ref=far_sums.at[f, k],
            send_sem=sum_send.at[f, k],
            recv_sem=sum_recv.at[f, k],
            device_id={"grp": lax.rem(z + k, nz)},
            device_id_type=MESH,
        )

    def ret_copy(k):
        return pltpu.make_async_remote_copy(
            src_ref=ret.at[block_rows(k)],
            dst_ref=back.at[block_rows(k)],
            send_sem=ret_send.at[k],
            recv_sem=ret_recv.at[k],
            device_id={"ep": lax.rem(me + ne - k, ne)},
            device_id_type=MESH,
        )

    def compute(f):
        x = rows[:, 0:model]
        dy = rows[:, model : 2 * model]
        gate = rows[:, 2 * model : 2 * model + LANES].astype(f32)
        full = weights[f].reshape(model, width3)
        pre = jnp.dot(x, full[:, 0 : 2 * width], preferred_element_type=f32)
        upstream = jnp.dot(dy, full[:, 2 * width :], preferred_element_type=f32)
        a, b = pre[:, :width], pre[:, width:]
        sig = jax.nn.sigmoid(a)
        silu = a * sig
        hidden = (silu * b).astype(bf16)
        hidden_f = hidden.astype(f32)
        gate_part = upstream * hidden_f
        if f == 0:
            gate_acc[...] = gate_part
        else:
            gate_acc[...] += gate_part
        hidden_grad = gate * upstream
        da = hidden_grad * b * sig * (1.0 + a * (1.0 - sig))
        db = hidden_grad * silu
        pre_grad = jnp.concatenate([da, db], axis=1).astype(bf16)
        gated = (gate * hidden_f).astype(bf16)

        @pl.loop(0, nz)
        def _(g):
            here = pl.ds(pl.multiple_of(g * shard, shard), shard)
            gu = jnp.dot(x_t[here, :], pre_grad, preferred_element_type=f32).astype(bf16)
            dn = jnp.dot(dy_t[here, :], gated, preferred_element_type=f32).astype(bf16)
            slot_grads[f, :, g, :, 0 : 2 * width] = gu.reshape(ne, own_rows, 2 * width)
            slot_grads[f, :, g, :, 2 * width :] = dn.reshape(ne, own_rows, width)

        for k in range(1, ne):
            grad_copy(f, k).start()

        @pl.loop(0, nz)
        def _(g):
            here = pl.ds(pl.multiple_of(g * shard, shard), shard)
            part = lax.dot_general(
                pre_grad,
                weights[f, g, :, 0 : 2 * width],
                (((1,), (1,)), ((), ())),
                preferred_element_type=f32,
            )
            if f == 0:
                row_acc[:, here] = part
            elif f < chunks - 1:
                row_acc[:, here] += part
            else:
                ret[:, here] = (row_acc[:, here] + part).astype(bf16)

    def plane_sum(f):
        for k in range(1, ne):
            grad_copy(f, k).wait_recv()

        @pl.loop(0, nz)
        def _(g):
            @pl.loop(0, own_rows // ROW_TILE)
            def _(r):
                here = pl.ds(pl.multiple_of(r * ROW_TILE, ROW_TILE), ROW_TILE)
                total = [None] * experts
                for k in range(ne):
                    if k == 0:
                        value = slot_grads[f, me, g, here, :].astype(f32)
                    else:
                        value = peer_grads[f, k, g, here, :].astype(f32)
                    for e in range(experts):
                        term = value * mask_ref[e, k]
                        total[e] = term if total[e] is None else total[e] + term
                for e in range(experts):
                    plane_sums[f, g, e, here, :] = total[e].astype(bf16)

        for k in range(1, nz):
            sum_copy(f, k).start()

    def finish(f):
        for k in range(1, nz):
            sum_copy(f, k).wait_recv()

        @pl.loop(0, experts)
        def _(e):
            total = plane_sums[f, z, e].astype(f32)
            for k in range(1, nz):
                total = total + far_sums[f, k, e].astype(f32)
            total = total / nz
            for part in range(3):
                start = part * hidden_width + f * width
                wgrad_ref[e, :, start : start + width] = total[
                    :, part * width : (part + 1) * width
                ]

    start_own(0)
    if chunks > 1:
        start_own(1)

    @pl.loop(1, ne)
    def _(k):
        pack(k, send_rows)
        out_copy(k).start()

    pack(0, rows)

    def rows_ready():
        for k in range(1, ne):
            out_copy(k).wait_recv()

        @pl.loop(0, model // LANES)
        def _(c):
            here = pl.ds(pl.multiple_of(c * LANES, LANES), LANES)
            there = pl.ds(pl.multiple_of(model + c * LANES, LANES), LANES)
            x_t[here, :] = rows[:, here].T
            dy_t[here, :] = rows[:, there].T

    def hop_range(f, low, high):
        for hop in range(low, min(high, nz)):
            arrive(f, hop)

    late = chunks > 1 and nz > 2
    hop_range(0, 1, nz)
    if not late:
        rows_ready()
        compute(0)
    for f in range(1, chunks):
        if f + 1 < chunks:
            start_own(f + 1)
        if f == 1 and late:
            hop_range(1, 1, nz - 1)
            rows_ready()
            compute(0)
            hop_range(1, nz - 1, nz)
        else:
            hop_range(f, 1, nz - 1)
            if f >= 2:
                plane_sum(f - 2)
            hop_range(f, nz - 1, nz)
        compute(f)

    ret[:, model : model + LANES] = jnp.broadcast_to(
        jnp.sum(gate_acc[...], axis=1, keepdims=True), (count, LANES)
    ).astype(bf16)
    for k in range(1, ne):
        ret_copy(k).start()
    back[0:block, :] = ret[0:block, :]
    if chunks > 1:
        plane_sum(chunks - 2)
    for f in range(chunks - 2):
        finish(f)
    plane_sum(chunks - 1)

    for k in range(1, ne):
        ret_copy(k).wait_recv()
    first, second = unpack_ref[0], unpack_ref[1]
    both = first + second

    @pl.loop(0, nz)
    def _(g):
        here = pl.ds(pl.multiple_of(g * shard, shard), shard)
        tgrad_ref[:, here] = jnp.dot(
            both, back[:, here], preferred_element_type=f32
        ).astype(bf16)

    gates_back = back[:, model : model + LANES]
    lane = lax.broadcasted_iota(jnp.int32, ggrad_ref.shape, 1)
    ggrad_ref[...] = jnp.where(
        lane == 0,
        jnp.dot(first, gates_back, preferred_element_type=f32),
        jnp.dot(second, gates_back, preferred_element_type=f32),
    ).astype(bf16)

    for f in range(max(chunks - 2, 0), chunks):
        finish(f)

    shard_sends_done()
    for k in range(1, ne):
        out_copy(k).wait_send()
        ret_copy(k).wait_send()
    for f in range(chunks):
        for k in range(1, ne):
            grad_copy(f, k).wait_send()
        for k in range(1, nz):
            sum_copy(f, k).wait_send()


def fused(tokens, out_grad, routes, gates, w_gate_up, w_down, plan, failed):
    nz = lax.axis_size("grp")
    ne = lax.axis_size("ep")
    z = lax.axis_index("grp")
    me = lax.axis_index("ep")
    tok_count, model = tokens.shape
    topk = routes.shape[1]
    experts = ne // 2
    capacity = tok_count * topk * 5 // (4 * ne)
    block = -(-capacity // ROW_TILE) * ROW_TILE
    count = ne * block
    shard = w_gate_up.shape[1]
    hidden_width = w_down.shape[2]
    width = LANES
    chunks = hidden_width // width
    own_rows = model // (nz * ne)
    in_service = 1 - lax.dynamic_index_in_dim(failed, z, 0, keepdims=False)
    slot_index, slot_rank = assign(routes, plan, in_service, capacity, experts)
    place = (lax.rem(slot_index - me + ne, ne) * block + slot_rank).reshape(tok_count, topk).T
    spots = jnp.arange(count, dtype=jnp.int32)
    pack = (spots[None, :, None] == place[:, None, :]).astype(jnp.bfloat16)
    unpack = (spots[None, None, :] == place[:, :, None]).astype(jnp.bfloat16)
    gate_wide = jnp.broadcast_to(gates.T[:, :, None], (topk, tok_count, LANES))
    source = lax.rem(me - jnp.arange(ne, dtype=jnp.int32) + ne, ne)
    hosted = (plan[None, :] == jnp.arange(experts, dtype=jnp.int32)[:, None]) & (
        in_service[None, :] > 0
    )
    mask = hosted.astype(jnp.float32)[:, source]
    bf16, f32 = jnp.bfloat16, jnp.float32
    vmem = pl.BlockSpec(memory_space=pltpu.VMEM)
    dma = pltpu.SemaphoreType.DMA
    tgrad, ggrad, wgrad = pl.pallas_call(
        functools.partial(fused_kernel, nz, ne, block),
        out_shape=(
            jax.ShapeDtypeStruct((tok_count, model), bf16),
            jax.ShapeDtypeStruct((tok_count, LANES), bf16),
            jax.ShapeDtypeStruct((experts, own_rows, 3 * hidden_width), f32),
        ),
        in_specs=[vmem] * 7 + [pl.BlockSpec(memory_space=pltpu.SMEM)],
        out_specs=(vmem, vmem, vmem),
        scratch_shapes=[
            pltpu.VMEM((chunks, nz, shard, 3 * width), bf16),
            pltpu.VMEM((count, 2 * model + LANES), bf16),
            pltpu.VMEM((count, 2 * model + LANES), bf16),
            pltpu.VMEM((model, count), bf16),
            pltpu.VMEM((model, count), bf16),
            pltpu.VMEM((count, model), f32),
            pltpu.VMEM((count, width), f32),
            pltpu.VMEM((chunks, ne, nz, own_rows, 3 * width), bf16),
            pltpu.VMEM((chunks, ne, nz, own_rows, 3 * width), bf16),
            pltpu.VMEM((chunks, nz, experts, own_rows, 3 * width), bf16),
            pltpu.VMEM((chunks, nz, experts, own_rows, 3 * width), bf16),
            pltpu.VMEM((count, model + LANES), bf16),
            pltpu.VMEM((count, model + LANES), bf16),
            dma((chunks, nz, 2)),
            dma((chunks, nz)),
            dma((ne,)),
            dma((ne,)),
            dma((chunks, ne)),
            dma((chunks, ne)),
            dma((chunks, nz)),
            dma((chunks, nz)),
            dma((ne,)),
            dma((ne,)),
        ],
        compiler_params=pltpu.CompilerParams(
            collective_id=0, has_side_effects=True, vmem_limit_bytes=60 * 1024 * 1024
        ),
        cost_estimate=pl.CostEstimate(
            flops=18 * count * model * hidden_width,
            bytes_accessed=16 * 1024 * 1024,
            transcendentals=count * hidden_width,
        ),
    )(tokens, out_grad, pack, unpack, gate_wide, w_gate_up, w_down, mask)
    return (tgrad, ggrad[:, :topk], wgrad)


def local(tokens, out_grad, routes, gates, w_gate_up, w_down, plan, failed):
    groups = lax.axis_size("grp")
    slot_count = lax.axis_size("ep")
    my_group = lax.axis_index("grp")
    tok_count, model_width = tokens.shape
    topk_count = routes.shape[1]
    experts = slot_count // 2
    capacity = tok_count * topk_count * 5 // (4 * slot_count)
    route_count = tok_count * topk_count
    buffer_rows = slot_count * capacity
    in_service = 1 - lax.dynamic_index_in_dim(failed, my_group, 0, keepdims=False)
    slot_index, slot_rank = assign(routes, plan, in_service, capacity, experts)
    positions = slot_index * capacity + slot_rank
    source = (
        jnp.full((buffer_rows,), route_count, jnp.int32)
        .at[positions]
        .set(jnp.arange(route_count, dtype=jnp.int32))
    )
    token_of = source // topk_count
    zero_row = jnp.zeros((1, model_width), jnp.bfloat16)
    send_x = jnp.concatenate([tokens, zero_row], axis=0)[token_of].reshape(
        slot_count, capacity, model_width
    )
    send_dy = jnp.concatenate([out_grad, zero_row], axis=0)[token_of].reshape(
        slot_count, capacity, model_width
    )
    send_gate = jnp.concatenate([gates.reshape(route_count), jnp.zeros((1,), jnp.bfloat16)])[source]
    send_gate = send_gate.reshape(slot_count, capacity)
    recv_x, recv_dy, recv_gate = (
        lax.all_to_all(send_x, "ep", split_axis=0, concat_axis=0, tiled=True),
        lax.all_to_all(send_dy, "ep", split_axis=0, concat_axis=0, tiled=True),
        lax.all_to_all(send_gate, "ep", split_axis=0, concat_axis=0, tiled=True),
    )
    full_gu, full_dn = (
        lax.all_gather(w_gate_up, "grp", axis=1, tiled=True),
        lax.all_gather(w_down, "grp", axis=1, tiled=True),
    )
    full_gu = full_gu[0]
    full_dn = full_dn[0]
    hidden_width = full_dn.shape[1]
    flat_x = recv_x.reshape(buffer_rows, model_width)
    flat_dy = recv_dy.reshape(buffer_rows, model_width)
    flat_gate = recv_gate.reshape(buffer_rows)
    row_grads, gate_rows, grad_gu, grad_dn = expert_rows(
        flat_x, flat_dy, flat_gate, full_gu, full_dn
    )
    back_x, back_gate = (
        lax.all_to_all(
            row_grads.reshape(slot_count, capacity, model_width),
            "ep",
            split_axis=0,
            concat_axis=0,
            tiled=True,
        ),
        lax.all_to_all(
            gate_rows.reshape(slot_count, capacity), "ep", split_axis=0, concat_axis=0, tiled=True
        ),
    )
    route_rows = back_x.reshape(buffer_rows, model_width)[positions]
    token_grad = jnp.sum(
        route_rows.reshape(tok_count, topk_count, model_width).astype(jnp.float32), axis=1
    ).astype(jnp.bfloat16)
    gate_grad = back_gate.reshape(buffer_rows)[positions].reshape(tok_count, topk_count)
    columns = 3 * hidden_width
    rows_each = model_width // (groups * slot_count)
    slot_grad = jnp.concatenate([grad_gu, grad_dn], axis=1).astype(jnp.bfloat16)
    slot_grad = slot_grad.reshape(groups, slot_count, rows_each, columns)
    expert_ids = jnp.arange(experts, dtype=jnp.int32)
    mixed = lax.all_to_all(
        lax.all_to_all(slot_grad, "grp", split_axis=0, concat_axis=0, tiled=True),
        "ep",
        split_axis=1,
        concat_axis=1,
        tiled=True,
    )
    hosted_all = (
        (plan[None, None, :] == expert_ids[None, :, None]) & (failed[:, None, :] == 0)
    ).astype(jnp.bfloat16)
    per_group = jnp.einsum("ges,gsrc->gerc", hosted_all, mixed, preferred_element_type=jnp.float32)
    weight_grad = jnp.sum(per_group, axis=0) / groups
    return (token_grad, gate_grad, weight_grad)


def solution(mesh):
    nz, ne = mesh.shape["grp"], mesh.shape["ep"]

    def step(tokens, *others):
        aligned = tokens.shape[1] % (nz * ne * ROW_TILE) == 0
        return (fused if aligned else local)(tokens, *others)

    placed = (
        P(("grp", "ep"), None),
        P(("grp", "ep"), None),
        P(("grp", "ep"), None),
        P(("grp", "ep"), None),
        P("ep", "grp", None),
        P("ep", "grp", None),
        P(),
        P(),
    )
    return jax.shard_map(
        step,
        mesh=mesh,
        in_specs=placed,
        out_specs=(P(("grp", "ep"), None), P(("grp", "ep"), None), P(None, ("grp", "ep"), None)),
        check_vma=False,
    )
```

```python
import functools

import jax
import jax.numpy as jnp
from jax import lax
from jax.experimental import pallas as pl
from jax.experimental.pallas import tpu as pltpu
from jax.sharding import PartitionSpec as P


def assign(route_ids, hosting, in_service, capacity, experts):
    route_count = route_ids.shape[0] * route_ids.shape[1]
    slot_count = hosting.shape[0]
    flat_routes = route_ids.reshape(route_count)
    expert_ids = jnp.arange(experts, dtype=jnp.int32)
    hosted = ((hosting[None, :] == expert_ids[:, None]) & (in_service[None, :] > 0)).astype(
        jnp.int32
    )
    replicas = jnp.sum(hosted, axis=1)
    ordinal = jnp.sum(hosted * (jnp.cumsum(hosted, axis=1) - 1), axis=0)
    expert_hot = (flat_routes[:, None] == expert_ids[None, :]).astype(jnp.int32)
    expert_rank = jnp.sum(expert_hot * (jnp.cumsum(expert_hot, axis=0) - 1), axis=1)
    route_replicas = jnp.sum(expert_hot * replicas[None, :], axis=1)
    replica_pick = expert_rank % route_replicas
    slot_hot = (
        (hosting[None, :] == flat_routes[:, None])
        & (in_service[None, :] > 0)
        & (ordinal[None, :] == replica_pick[:, None])
    ).astype(jnp.int32)
    slot_rank = jnp.sum(slot_hot * (jnp.cumsum(slot_hot, axis=0) - 1), axis=1)
    slot_index = jnp.sum(slot_hot * jnp.arange(slot_count, dtype=jnp.int32)[None, :], axis=1)
    return slot_index, slot_rank


def expert_rows(rows_x, rows_dy, rows_gate, full_gu, full_dn):
    hidden_width = full_dn.shape[1]
    projected = jnp.dot(rows_x, full_gu, preferred_element_type=jnp.float32)
    gate_pre = projected[:, :hidden_width]
    up_pre = projected[:, hidden_width:]
    sigmoid_a = jax.nn.sigmoid(gate_pre)
    silu_a = gate_pre * sigmoid_a
    hidden = (silu_a * up_pre).astype(jnp.bfloat16)
    upstream = jnp.dot(rows_dy, full_dn, preferred_element_type=jnp.float32)
    rebuilt = lax.dot_general(
        hidden, full_dn, (((1,), (1,)), ((), ())), preferred_element_type=jnp.float32
    )
    gate_grad = jnp.sum(rows_dy.astype(jnp.float32) * rebuilt, axis=1).astype(jnp.bfloat16)
    gate_value = rows_gate.astype(jnp.float32)[:, None]
    hidden_grad = gate_value * upstream
    gate_delta = hidden_grad * up_pre * sigmoid_a * (1.0 + gate_pre * (1.0 - sigmoid_a))
    up_delta = hidden_grad * silu_a
    pre_grad = jnp.concatenate([gate_delta, up_delta], axis=1).astype(jnp.bfloat16)
    row_grad = lax.dot_general(
        pre_grad, full_gu, (((1,), (1,)), ((), ())), preferred_element_type=jnp.float32
    ).astype(jnp.bfloat16)
    gated_hidden = (gate_value * hidden.astype(jnp.float32)).astype(jnp.bfloat16)
    grad_gu = lax.dot_general(
        rows_x, pre_grad, (((0,), (0,)), ((), ())), preferred_element_type=jnp.float32
    )
    grad_dn = lax.dot_general(
        rows_dy, gated_hidden, (((0,), (0,)), ((), ())), preferred_element_type=jnp.float32
    )
    return (row_grad, gate_grad, grad_gu, grad_dn)


MESH = pl.DeviceIdType.MESH
LANES = 128
ROW_TILE = 16


def fused_kernel(
    nz, ne, block,
    tok_ref, dy_ref, route_ref, gate_ref, gu_ref, dn_ref, plan_ref, failed_ref,
    tgrad_ref, ggrad_ref, wgrad_ref,
    weights, send_rows, rows, x_t, dy_t, row_acc, gate_acc, slot_grads, peer_grads,
    plane_sums, from_below, from_above, ret, back, pack_ref, unpack_ref,
    ag_send, ag_recv, out_send, out_recv, grad_send, grad_recv, sum_send, sum_recv,
    ret_send, ret_recv,
):
    z = lax.axis_index("grp")
    me = lax.axis_index("ep")
    chunks, _, shard, width3 = weights.shape
    model = nz * shard
    width = width3 // 3
    hidden_width = chunks * width
    experts = wgrad_ref.shape[0]
    own_rows = wgrad_ref.shape[1]
    count = ne * block
    f32, bf16 = jnp.float32, jnp.bfloat16

    barrier = pltpu.get_barrier_semaphore()
    for k in range(1, ne):
        pl.semaphore_signal(
            barrier, inc=1, device_id={"ep": lax.rem(me + k, ne)}, device_id_type=MESH
        )
    for k in range(1, nz):
        pl.semaphore_signal(
            barrier, inc=1, device_id={"grp": lax.rem(z + k, nz)}, device_id_type=MESH
        )

    def stage(f):
        cols = slice(f * width, (f + 1) * width)
        up_cols = slice(hidden_width + f * width, hidden_width + (f + 1) * width)
        weights[f, z, :, 0:width] = gu_ref[0, :, cols]
        weights[f, z, :, width : 2 * width] = gu_ref[0, :, up_cols]
        weights[f, z, :, 2 * width : 3 * width] = dn_ref[0, :, cols]

    stage(0)
    pl.semaphore_wait(barrier, ne - 1 + nz - 1)

    def shard_copy(f, owner, up):
        step = 1 if up else nz - 1
        return pltpu.make_async_remote_copy(
            src_ref=weights.at[f, owner],
            dst_ref=weights.at[f, owner],
            send_sem=ag_send.at[f, owner, 0 if up else 1],
            recv_sem=ag_recv.at[f, owner],
            device_id={"grp": lax.rem(z + step, nz)},
            device_id_type=MESH,
        )

    def start_own(f):
        @pl.when(z < nz - 1)
        def _():
            shard_copy(f, z, True).start()

        @pl.when(z > 0)
        def _():
            shard_copy(f, z, False).start()

    def arrive(f, hop):
        @pl.when(z >= hop)
        def _():
            shard_copy(f, z - hop, True).wait_recv()

            @pl.when(z < nz - 1)
            def _():
                shard_copy(f, z - hop, True).start()

        @pl.when(z + hop < nz)
        def _():
            shard_copy(f, z + hop, False).wait_recv()

            @pl.when(z > 0)
            def _():
                shard_copy(f, z + hop, False).start()

    def shard_sends_done():
        for f in range(chunks):
            for hop in range(nz):
                @pl.when((z >= hop) & (z < nz - 1))
                def _():
                    shard_copy(f, z - hop, True).wait_send()

                @pl.when((z + hop < nz) & (z > 0))
                def _():
                    shard_copy(f, z + hop, False).wait_send()

    def block_rows(k):
        return pl.ds(pl.multiple_of(k * block, ROW_TILE), block)

    def out_copy(k):
        return pltpu.make_async_remote_copy(
            src_ref=send_rows.at[block_rows(k)],
            dst_ref=rows.at[block_rows(k)],
            send_sem=out_send.at[k],
            recv_sem=out_recv.at[k],
            device_id={"ep": lax.rem(me + k, ne)},
            device_id_type=MESH,
        )

    def pack(k, target):
        here = block_rows(k)
        first, second = pack_ref[0, here, :], pack_ref[1, here, :]
        both = first + second
        target[here, 0:model] = jnp.dot(
            both, tok_ref[...], preferred_element_type=f32
        ).astype(bf16)
        target[here, model : 2 * model] = jnp.dot(
            both, dy_ref[...], preferred_element_type=f32
        ).astype(bf16)
        target[here, 2 * model : 2 * model + LANES] = (
            jnp.dot(first, gate_wide[0], preferred_element_type=f32)
            + jnp.dot(second, gate_wide[1], preferred_element_type=f32)
        ).astype(bf16)

    def grad_copy(f, k):
        return pltpu.make_async_remote_copy(
            src_ref=slot_grads.at[f, lax.rem(me + k, ne)],
            dst_ref=peer_grads.at[f, k],
            send_sem=grad_send.at[f, k],
            recv_sem=grad_recv.at[f, k],
            device_id={"ep": lax.rem(me + k, ne)},
            device_id_type=MESH,
        )

    def sum_copy(f, dest, up):
        step = 1 if up else nz - 1
        target = from_below if up else from_above
        return pltpu.make_async_remote_copy(
            src_ref=plane_sums.at[f, dest],
            dst_ref=target.at[f, dest],
            send_sem=sum_send.at[f, dest],
            recv_sem=sum_recv.at[f, dest, 0 if up else 1],
            device_id={"grp": lax.rem(z + step, nz)},
            device_id_type=MESH,
        )

    def sum_hop(f, turn):
        for up in (True, False):
            dest = nz - 1 - turn if up else turn
            incoming = from_below if up else from_above

            @pl.when((z > 0) & (z < dest) if up else (z < nz - 1) & (z > dest))
            def _():
                sum_copy(f, dest, up).wait_recv()

                @pl.loop(0, experts)
                def _(e):
                    plane_sums[f, dest, e] = (
                        plane_sums[f, dest, e].astype(f32) + incoming[f, dest, e].astype(f32)
                    ).astype(bf16)

            @pl.when(z < dest if up else z > dest)
            def _():
                sum_copy(f, dest, up).start()

    def ret_copy(k):
        return pltpu.make_async_remote_copy(
            src_ref=ret.at[block_rows(k)],
            dst_ref=back.at[block_rows(k)],
            send_sem=ret_send.at[k],
            recv_sem=ret_recv.at[k],
            device_id={"ep": lax.rem(me + ne - k, ne)},
            device_id_type=MESH,
        )

    def compute(f):
        x = rows[:, 0:model]
        dy = rows[:, model : 2 * model]
        gate = rows[:, 2 * model : 2 * model + LANES].astype(f32)
        full = weights[f].reshape(model, width3)
        pre = jnp.dot(x, full[:, 0 : 2 * width], preferred_element_type=f32)
        upstream = jnp.dot(dy, full[:, 2 * width :], preferred_element_type=f32)
        a, b = pre[:, :width], pre[:, width:]
        sig = jax.nn.sigmoid(a)
        silu = a * sig
        hidden = (silu * b).astype(bf16)
        hidden_f = hidden.astype(f32)
        gate_part = upstream * hidden_f
        if f == 0:
            gate_acc[...] = gate_part
        else:
            gate_acc[...] += gate_part
        hidden_grad = gate * upstream
        da = hidden_grad * b * sig * (1.0 + a * (1.0 - sig))
        db = hidden_grad * silu
        pre_grad = jnp.concatenate([da, db], axis=1).astype(bf16)
        gated = (gate * hidden_f).astype(bf16)

        @pl.loop(0, nz)
        def _(g):
            here = pl.ds(pl.multiple_of(g * shard, shard), shard)
            gu = jnp.dot(x_t[here, :], pre_grad, preferred_element_type=f32).astype(bf16)
            dn = jnp.dot(dy_t[here, :], gated, preferred_element_type=f32).astype(bf16)
            slot_grads[f, :, g, :, 0 : 2 * width] = gu.reshape(ne, own_rows, 2 * width)
            slot_grads[f, :, g, :, 2 * width :] = dn.reshape(ne, own_rows, width)

        for k in range(1, ne):
            grad_copy(f, k).start()

        @pl.loop(0, nz)
        def _(g):
            here = pl.ds(pl.multiple_of(g * shard, shard), shard)
            part = lax.dot_general(
                pre_grad,
                weights[f, g, :, 0 : 2 * width],
                (((1,), (1,)), ((), ())),
                preferred_element_type=f32,
            )
            if f == 0:
                row_acc[:, here] = part
            elif f < chunks - 1:
                row_acc[:, here] += part
            else:
                ret[:, here] = (row_acc[:, here] + part).astype(bf16)

    def plane_sum(f):
        for k in range(1, ne):
            grad_copy(f, k).wait_recv()

        @pl.loop(0, nz)
        def _(g):
            @pl.loop(0, own_rows // ROW_TILE)
            def _(r):
                here = pl.ds(pl.multiple_of(r * ROW_TILE, ROW_TILE), ROW_TILE)
                total = [None] * experts
                for k in range(ne):
                    if k == 0:
                        value = slot_grads[f, me, g, here, :].astype(f32)
                    else:
                        value = peer_grads[f, k, g, here, :].astype(f32)
                    for e in range(experts):
                        term = value * mask[e][k]
                        total[e] = term if total[e] is None else total[e] + term
                for e in range(experts):
                    plane_sums[f, g, e, here, :] = total[e].astype(bf16)

    def finish(f):
        def add(incoming, first):
            @pl.loop(0, experts)
            def _(e):
                value = incoming[f, z, e].astype(f32)
                if first:
                    value = value + plane_sums[f, z, e].astype(f32)
                for part in range(3):
                    start = part * hidden_width + f * width
                    here = value[:, part * width : (part + 1) * width] / nz
                    if first:
                        wgrad_ref[e, :, start : start + width] = here
                    else:
                        wgrad_ref[e, :, start : start + width] += here

        @pl.when(z > 0)
        def _():
            sum_copy(f, z, True).wait_recv()
            add(from_below, True)

        @pl.when((z > 0) & (z < nz - 1))
        def _():
            sum_copy(f, z, False).wait_recv()
            add(from_above, False)

        @pl.when(z == 0)
        def _():
            sum_copy(f, z, False).wait_recv()
            add(from_above, True)

    start_own(0)
    for f in range(1, chunks):
        stage(f)
    if chunks > 1:
        start_own(1)

    live = [1 - failed_ref[z, s] for s in range(ne)]
    tokens_here = tok_ref.shape[0]
    square = (tokens_here, LANES)
    lane = lax.broadcasted_iota(jnp.int32, square, 1)
    hosts_row = lax.broadcasted_iota(jnp.int32, (LANES, LANES), 0)
    hosts_lane = lax.broadcasted_iota(jnp.int32, (LANES, LANES), 1)
    hosts = jnp.zeros((LANES, LANES), f32)
    replicas = jnp.zeros(square, f32)
    ordinal = jnp.zeros(square, f32)
    for s in range(ne):
        served = live[s].astype(f32)
        hosts += jnp.where(
            (hosts_row == plan_ref[s]) & (hosts_lane == s), served, 0.0
        )
        replicas += jnp.where(lane == plan_ref[s], served, 0.0)
        before = jnp.int32(0)
        for other in range(s):
            before += (plan_ref[other] == plan_ref[s]).astype(jnp.int32) * live[other]
        ordinal += jnp.where(lane == s, before.astype(f32), 0.0)
    hosts = hosts.astype(bf16)
    earlier = (
        lax.broadcasted_iota(jnp.int32, (tokens_here, tokens_here), 1)
        < lax.broadcasted_iota(jnp.int32, (tokens_here, tokens_here), 0)
    ).astype(f32).astype(bf16)
    wanted = [
        (lane == route_ref[:, k : k + 1]).astype(f32) for k in range(2)
    ]
    ranks = jnp.dot(earlier, (wanted[0] + wanted[1]).astype(bf16), preferred_element_type=f32)
    chosen = []
    for k in range(2):
        rank = jnp.sum(wanted[k] * ranks, axis=1, keepdims=True)
        n = jnp.sum(wanted[k] * replicas, axis=1, keepdims=True)
        pick = rank - n * jnp.floor((rank + 0.5) / n)
        hosting = jnp.dot(wanted[k].astype(bf16), hosts, preferred_element_type=f32)
        chosen.append(jnp.where(jnp.abs(ordinal - pick) < 0.5, hosting, 0.0))
    places = jnp.dot(earlier, (chosen[0] + chosen[1]).astype(bf16), preferred_element_type=f32)
    offset = (lax.rem(lane - me + ne, ne) * block).astype(f32)
    spot = lax.broadcasted_iota(jnp.int32, (tokens_here, count), 1)
    gate_wide = []
    for k in range(2):
        place = jnp.sum(
            jnp.where(lane < ne, chosen[k] * (places + offset), 0.0), axis=1, keepdims=True
        )
        hot = (spot == place.astype(jnp.int32)).astype(f32)
        unpack_ref[k] = hot.astype(bf16)
        pack_ref[k] = hot.T.astype(bf16)
        gate_wide.append(
            jnp.broadcast_to(gate_ref[:, k : k + 1].astype(f32), square).astype(bf16)
        )
    mask = []
    for e in range(experts):
        mask.append([])
        for k in range(ne):
            slot = lax.rem(me - k + ne, ne)
            hosted = (plan_ref[slot] == e).astype(jnp.int32) * (1 - failed_ref[z, slot])
            mask[e].append(hosted.astype(f32))

    @pl.loop(1, ne)
    def _(k):
        pack(k, send_rows)
        out_copy(k).start()

    pack(0, rows)

    def rows_ready():
        for k in range(1, ne):
            out_copy(k).wait_recv()

        @pl.loop(0, model // LANES)
        def _(c):
            here = pl.ds(pl.multiple_of(c * LANES, LANES), LANES)
            there = pl.ds(pl.multiple_of(model + c * LANES, LANES), LANES)
            x_t[here, :] = rows[:, here].T
            dy_t[here, :] = rows[:, there].T

    def hop_range(f, low, high):
        for hop in range(low, min(high, nz)):
            arrive(f, hop)

    turns = nz - 1
    duties = []

    def sums(f):
        return [functools.partial(plane_sum, f)] + [
            functools.partial(sum_hop, f, turn) for turn in range(turns)
        ]

    def work(most):
        for _ in range(min(most, len(duties))):
            duties.pop(0)()

    hop_range(0, 1, nz)
    for f in range(1, chunks):
        if f + 1 < chunks:
            start_own(f + 1)
        hop_range(f, 1, 2)
        work(1)
        hop_range(f, 2, nz - 1)
        if f == 1:
            rows_ready()
            compute(0)
        else:
            duties += sums(f - 2)
            work(2)
        hop_range(f, max(2, nz - 1), nz)
        work(1)
        compute(f)

    ret[:, model : model + LANES] = jnp.broadcast_to(
        jnp.sum(gate_acc[...], axis=1, keepdims=True), (count, LANES)
    ).astype(bf16)
    for k in range(1, ne):
        ret_copy(k).start()
    back[0:block, :] = ret[0:block, :]
    work(len(duties))
    for f in range(max(chunks - 2, 0), chunks - 1):
        for duty in sums(f):
            duty()
    for f in range(chunks - 1):
        finish(f)
    for duty in sums(chunks - 1):
        duty()

    for k in range(1, ne):
        ret_copy(k).wait_recv()
    first, second = unpack_ref[0], unpack_ref[1]
    both = first + second

    @pl.loop(0, nz)
    def _(g):
        here = pl.ds(pl.multiple_of(g * shard, shard), shard)
        tgrad_ref[:, here] = jnp.dot(
            both, back[:, here], preferred_element_type=f32
        ).astype(bf16)

    gates_back = back[:, model : model + LANES]
    ggrad_ref[...] = jnp.where(
        lane == 0,
        jnp.dot(first, gates_back, preferred_element_type=f32),
        jnp.dot(second, gates_back, preferred_element_type=f32),
    ).astype(bf16)

    finish(chunks - 1)

    shard_sends_done()
    for k in range(1, ne):
        out_copy(k).wait_send()
        ret_copy(k).wait_send()
    for f in range(chunks):
        for k in range(1, ne):
            grad_copy(f, k).wait_send()
        for dest in range(nz):
            for up in (True, False):
                @pl.when(z < dest if up else z > dest)
                def _():
                    sum_copy(f, dest, up).wait_send()


def fused(tokens, out_grad, routes, gates, w_gate_up, w_down, plan, failed):
    nz = lax.axis_size("grp")
    ne = lax.axis_size("ep")
    tok_count, model = tokens.shape
    topk = routes.shape[1]
    experts = ne // 2
    capacity = tok_count * topk * 5 // (4 * ne)
    block = -(-capacity // ROW_TILE) * ROW_TILE
    count = ne * block
    shard = w_gate_up.shape[1]
    hidden_width = w_down.shape[2]
    width = LANES
    chunks = hidden_width // width
    own_rows = model // (nz * ne)
    bf16, f32 = jnp.bfloat16, jnp.float32
    vmem = pl.BlockSpec(memory_space=pltpu.VMEM)
    dma = pltpu.SemaphoreType.DMA
    tgrad, ggrad, wgrad = pl.pallas_call(
        functools.partial(fused_kernel, nz, ne, block),
        out_shape=(
            jax.ShapeDtypeStruct((tok_count, model), bf16),
            jax.ShapeDtypeStruct((tok_count, LANES), bf16),
            jax.ShapeDtypeStruct((experts, own_rows, 3 * hidden_width), f32),
        ),
        in_specs=[vmem] * 6 + [pl.BlockSpec(memory_space=pltpu.SMEM)] * 2,
        out_specs=(vmem, vmem, vmem),
        scratch_shapes=[
            pltpu.VMEM((chunks, nz, shard, 3 * width), bf16),
            pltpu.VMEM((count, 2 * model + LANES), bf16),
            pltpu.VMEM((count, 2 * model + LANES), bf16),
            pltpu.VMEM((model, count), bf16),
            pltpu.VMEM((model, count), bf16),
            pltpu.VMEM((count, model), f32),
            pltpu.VMEM((count, width), f32),
            pltpu.VMEM((chunks, ne, nz, own_rows, 3 * width), bf16),
            pltpu.VMEM((chunks, ne, nz, own_rows, 3 * width), bf16),
            pltpu.VMEM((chunks, nz, experts, own_rows, 3 * width), bf16),
            pltpu.VMEM((chunks, nz, experts, own_rows, 3 * width), bf16),
            pltpu.VMEM((chunks, nz, experts, own_rows, 3 * width), bf16),
            pltpu.VMEM((count, model + LANES), bf16),
            pltpu.VMEM((count, model + LANES), bf16),
            pltpu.VMEM((topk, count, tok_count), bf16),
            pltpu.VMEM((topk, tok_count, count), bf16),
            dma((chunks, nz, 2)),
            dma((chunks, nz)),
            dma((ne,)),
            dma((ne,)),
            dma((chunks, ne)),
            dma((chunks, ne)),
            dma((chunks, nz)),
            dma((chunks, nz, 2)),
            dma((ne,)),
            dma((ne,)),
        ],
        compiler_params=pltpu.CompilerParams(
            collective_id=0, has_side_effects=True, vmem_limit_bytes=60 * 1024 * 1024
        ),
        cost_estimate=pl.CostEstimate(
            flops=18 * count * model * hidden_width,
            bytes_accessed=16 * 1024 * 1024,
            transcendentals=count * hidden_width,
        ),
    )(tokens, out_grad, routes, gates, w_gate_up, w_down, plan, failed)
    return (tgrad, ggrad[:, :topk], wgrad)


def local(tokens, out_grad, routes, gates, w_gate_up, w_down, plan, failed):
    groups = lax.axis_size("grp")
    slot_count = lax.axis_size("ep")
    my_group = lax.axis_index("grp")
    tok_count, model_width = tokens.shape
    topk_count = routes.shape[1]
    experts = slot_count // 2
    capacity = tok_count * topk_count * 5 // (4 * slot_count)
    route_count = tok_count * topk_count
    buffer_rows = slot_count * capacity
    in_service = 1 - lax.dynamic_index_in_dim(failed, my_group, 0, keepdims=False)
    slot_index, slot_rank = assign(routes, plan, in_service, capacity, experts)
    positions = slot_index * capacity + slot_rank
    source = (
        jnp.full((buffer_rows,), route_count, jnp.int32)
        .at[positions]
        .set(jnp.arange(route_count, dtype=jnp.int32))
    )
    token_of = source // topk_count
    zero_row = jnp.zeros((1, model_width), jnp.bfloat16)
    send_x = jnp.concatenate([tokens, zero_row], axis=0)[token_of].reshape(
        slot_count, capacity, model_width
    )
    send_dy = jnp.concatenate([out_grad, zero_row], axis=0)[token_of].reshape(
        slot_count, capacity, model_width
    )
    send_gate = jnp.concatenate([gates.reshape(route_count), jnp.zeros((1,), jnp.bfloat16)])[source]
    send_gate = send_gate.reshape(slot_count, capacity)
    recv_x, recv_dy, recv_gate = (
        lax.all_to_all(send_x, "ep", split_axis=0, concat_axis=0, tiled=True),
        lax.all_to_all(send_dy, "ep", split_axis=0, concat_axis=0, tiled=True),
        lax.all_to_all(send_gate, "ep", split_axis=0, concat_axis=0, tiled=True),
    )
    full_gu, full_dn = (
        lax.all_gather(w_gate_up, "grp", axis=1, tiled=True),
        lax.all_gather(w_down, "grp", axis=1, tiled=True),
    )
    full_gu = full_gu[0]
    full_dn = full_dn[0]
    hidden_width = full_dn.shape[1]
    flat_x = recv_x.reshape(buffer_rows, model_width)
    flat_dy = recv_dy.reshape(buffer_rows, model_width)
    flat_gate = recv_gate.reshape(buffer_rows)
    row_grads, gate_rows, grad_gu, grad_dn = expert_rows(
        flat_x, flat_dy, flat_gate, full_gu, full_dn
    )
    back_x, back_gate = (
        lax.all_to_all(
            row_grads.reshape(slot_count, capacity, model_width),
            "ep",
            split_axis=0,
            concat_axis=0,
            tiled=True,
        ),
        lax.all_to_all(
            gate_rows.reshape(slot_count, capacity), "ep", split_axis=0, concat_axis=0, tiled=True
        ),
    )
    route_rows = back_x.reshape(buffer_rows, model_width)[positions]
    token_grad = jnp.sum(
        route_rows.reshape(tok_count, topk_count, model_width).astype(jnp.float32), axis=1
    ).astype(jnp.bfloat16)
    gate_grad = back_gate.reshape(buffer_rows)[positions].reshape(tok_count, topk_count)
    columns = 3 * hidden_width
    rows_each = model_width // (groups * slot_count)
    slot_grad = jnp.concatenate([grad_gu, grad_dn], axis=1).astype(jnp.bfloat16)
    slot_grad = slot_grad.reshape(groups, slot_count, rows_each, columns)
    expert_ids = jnp.arange(experts, dtype=jnp.int32)
    mixed = lax.all_to_all(
        lax.all_to_all(slot_grad, "grp", split_axis=0, concat_axis=0, tiled=True),
        "ep",
        split_axis=1,
        concat_axis=1,
        tiled=True,
    )
    hosted_all = (
        (plan[None, None, :] == expert_ids[None, :, None]) & (failed[:, None, :] == 0)
    ).astype(jnp.bfloat16)
    per_group = jnp.einsum("ges,gsrc->gerc", hosted_all, mixed, preferred_element_type=jnp.float32)
    weight_grad = jnp.sum(per_group, axis=0) / groups
    return (token_grad, gate_grad, weight_grad)


def solution(mesh):
    nz, ne = mesh.shape["grp"], mesh.shape["ep"]

    def step(tokens, *others):
        aligned = tokens.shape[1] % (nz * ne * ROW_TILE) == 0
        return (fused if aligned else local)(tokens, *others)

    placed = (
        P(("grp", "ep"), None),
        P(("grp", "ep"), None),
        P(("grp", "ep"), None),
        P(("grp", "ep"), None),
        P("ep", "grp", None),
        P("ep", "grp", None),
        P(),
        P(),
    )
    return jax.shard_map(
        step,
        mesh=mesh,
        in_specs=placed,
        out_specs=(P(("grp", "ep"), None), P(("grp", "ep"), None), P(None, ("grp", "ep"), None)),
        check_vma=False,
    )
```

```python
import functools

import jax
import jax.numpy as jnp
from jax import lax
from jax.experimental import pallas as pl
from jax.experimental.pallas import tpu as pltpu
from jax.sharding import PartitionSpec as P


def assign(route_ids, hosting, in_service, capacity, experts):
    route_count = route_ids.shape[0] * route_ids.shape[1]
    slot_count = hosting.shape[0]
    flat_routes = route_ids.reshape(route_count)
    expert_ids = jnp.arange(experts, dtype=jnp.int32)
    hosted = ((hosting[None, :] == expert_ids[:, None]) & (in_service[None, :] > 0)).astype(
        jnp.int32
    )
    replicas = jnp.sum(hosted, axis=1)
    ordinal = jnp.sum(hosted * (jnp.cumsum(hosted, axis=1) - 1), axis=0)
    expert_hot = (flat_routes[:, None] == expert_ids[None, :]).astype(jnp.int32)
    expert_rank = jnp.sum(expert_hot * (jnp.cumsum(expert_hot, axis=0) - 1), axis=1)
    route_replicas = jnp.sum(expert_hot * replicas[None, :], axis=1)
    replica_pick = expert_rank % route_replicas
    slot_hot = (
        (hosting[None, :] == flat_routes[:, None])
        & (in_service[None, :] > 0)
        & (ordinal[None, :] == replica_pick[:, None])
    ).astype(jnp.int32)
    slot_rank = jnp.sum(slot_hot * (jnp.cumsum(slot_hot, axis=0) - 1), axis=1)
    slot_index = jnp.sum(slot_hot * jnp.arange(slot_count, dtype=jnp.int32)[None, :], axis=1)
    return slot_index, slot_rank


def expert_rows(rows_x, rows_dy, rows_gate, full_gu, full_dn):
    hidden_width = full_dn.shape[1]
    projected = jnp.dot(rows_x, full_gu, preferred_element_type=jnp.float32)
    gate_pre = projected[:, :hidden_width]
    up_pre = projected[:, hidden_width:]
    sigmoid_a = jax.nn.sigmoid(gate_pre)
    silu_a = gate_pre * sigmoid_a
    hidden = (silu_a * up_pre).astype(jnp.bfloat16)
    upstream = jnp.dot(rows_dy, full_dn, preferred_element_type=jnp.float32)
    rebuilt = lax.dot_general(
        hidden, full_dn, (((1,), (1,)), ((), ())), preferred_element_type=jnp.float32
    )
    gate_grad = jnp.sum(rows_dy.astype(jnp.float32) * rebuilt, axis=1).astype(jnp.bfloat16)
    gate_value = rows_gate.astype(jnp.float32)[:, None]
    hidden_grad = gate_value * upstream
    gate_delta = hidden_grad * up_pre * sigmoid_a * (1.0 + gate_pre * (1.0 - sigmoid_a))
    up_delta = hidden_grad * silu_a
    pre_grad = jnp.concatenate([gate_delta, up_delta], axis=1).astype(jnp.bfloat16)
    row_grad = lax.dot_general(
        pre_grad, full_gu, (((1,), (1,)), ((), ())), preferred_element_type=jnp.float32
    ).astype(jnp.bfloat16)
    gated_hidden = (gate_value * hidden.astype(jnp.float32)).astype(jnp.bfloat16)
    grad_gu = lax.dot_general(
        rows_x, pre_grad, (((0,), (0,)), ((), ())), preferred_element_type=jnp.float32
    )
    grad_dn = lax.dot_general(
        rows_dy, gated_hidden, (((0,), (0,)), ((), ())), preferred_element_type=jnp.float32
    )
    return (row_grad, gate_grad, grad_gu, grad_dn)


MESH = pl.DeviceIdType.MESH
LANES = 128
ROW_TILE = 16


def fused_kernel(
    nz, ne, block,
    tok_ref, dy_ref, route_ref, gate_ref, gu_ref, dn_ref, plan_ref, failed_ref,
    tgrad_ref, ggrad_ref, wgrad_ref,
    weights, send_rows, rows, x_t, dy_t, row_acc, gate_acc, slot_grads, peer_grads,
    plane_sums, from_below, from_above, ret, back, pack_ref, unpack_ref,
    ag_send, ag_recv, out_send, out_recv, grad_send, grad_recv, sum_send, sum_recv,
    ret_send, ret_recv,
):
    z = lax.axis_index("grp")
    me = lax.axis_index("ep")
    chunks, _, shard, width3 = weights.shape
    model = nz * shard
    width = width3 // 3
    hidden_width = chunks * width
    experts = wgrad_ref.shape[0]
    own_rows = wgrad_ref.shape[1]
    count = ne * block
    f32, bf16 = jnp.float32, jnp.bfloat16
    last = chunks - 1
    both_parts, gu_part, dn_part = (0, width3), (0, 2 * width), (2 * width, width3)
    weight_pieces = [(f,) + both_parts for f in range(last)]
    weight_pieces += [(last,) + gu_part, (last,) + dn_part]
    grad_pieces = [(f,) + both_parts for f in range(last)]
    grad_pieces += [(last,) + dn_part, (last,) + gu_part]

    barrier = pltpu.get_barrier_semaphore()
    for k in range(1, ne):
        pl.semaphore_signal(
            barrier, inc=1, device_id={"ep": lax.rem(me + k, ne)}, device_id_type=MESH
        )
    for k in range(1, nz):
        pl.semaphore_signal(
            barrier, inc=1, device_id={"grp": lax.rem(z + k, nz)}, device_id_type=MESH
        )

    def stage(f):
        cols = slice(f * width, (f + 1) * width)
        up_cols = slice(hidden_width + f * width, hidden_width + (f + 1) * width)
        weights[f, z, :, 0:width] = gu_ref[0, :, cols]
        weights[f, z, :, width : 2 * width] = gu_ref[0, :, up_cols]
        weights[f, z, :, 2 * width : 3 * width] = dn_ref[0, :, cols]

    stage(0)
    pl.semaphore_wait(barrier, ne - 1 + nz - 1)

    def shard_copy(p, owner, up):
        step = 1 if up else nz - 1
        f, low, high = weight_pieces[p]
        return pltpu.make_async_remote_copy(
            src_ref=weights.at[f, owner, :, low:high],
            dst_ref=weights.at[f, owner, :, low:high],
            send_sem=ag_send.at[p, owner, 0 if up else 1],
            recv_sem=ag_recv.at[p, owner],
            device_id={"grp": lax.rem(z + step, nz)},
            device_id_type=MESH,
        )

    def start_own(p):
        @pl.when(z < nz - 1)
        def _():
            shard_copy(p, z, True).start()

        @pl.when(z > 0)
        def _():
            shard_copy(p, z, False).start()

    def arrive(p, hop):
        @pl.when(z >= hop)
        def _():
            shard_copy(p, z - hop, True).wait_recv()

            @pl.when(z < nz - 1)
            def _():
                shard_copy(p, z - hop, True).start()

        @pl.when(z + hop < nz)
        def _():
            shard_copy(p, z + hop, False).wait_recv()

            @pl.when(z > 0)
            def _():
                shard_copy(p, z + hop, False).start()

    def shard_sends_done():
        for p in range(len(weight_pieces)):
            for hop in range(nz):
                @pl.when((z >= hop) & (z < nz - 1))
                def _():
                    shard_copy(p, z - hop, True).wait_send()

                @pl.when((z + hop < nz) & (z > 0))
                def _():
                    shard_copy(p, z + hop, False).wait_send()

    def block_rows(k):
        return pl.ds(pl.multiple_of(k * block, ROW_TILE), block)

    def out_copy(k):
        return pltpu.make_async_remote_copy(
            src_ref=send_rows.at[block_rows(k)],
            dst_ref=rows.at[block_rows(k)],
            send_sem=out_send.at[k],
            recv_sem=out_recv.at[k],
            device_id={"ep": lax.rem(me + k, ne)},
            device_id_type=MESH,
        )

    def pack(k, target):
        here = block_rows(k)
        first, second = pack_ref[0, here, :], pack_ref[1, here, :]
        both = first + second
        target[here, 0:model] = jnp.dot(
            both, tok_ref[...], preferred_element_type=f32
        ).astype(bf16)
        target[here, model : 2 * model] = jnp.dot(
            both, dy_ref[...], preferred_element_type=f32
        ).astype(bf16)
        target[here, 2 * model : 2 * model + LANES] = (
            jnp.dot(first, gate_wide[0], preferred_element_type=f32)
            + jnp.dot(second, gate_wide[1], preferred_element_type=f32)
        ).astype(bf16)

    def grad_copy(q, k):
        f, low, high = grad_pieces[q]
        return pltpu.make_async_remote_copy(
            src_ref=slot_grads.at[f, lax.rem(me + k, ne), :, :, low:high],
            dst_ref=peer_grads.at[f, k, :, :, low:high],
            send_sem=grad_send.at[q, k],
            recv_sem=grad_recv.at[q, k],
            device_id={"ep": lax.rem(me + k, ne)},
            device_id_type=MESH,
        )

    def sum_copy(q, dest, up):
        step = 1 if up else nz - 1
        target = from_below if up else from_above
        f, low, high = grad_pieces[q]
        return pltpu.make_async_remote_copy(
            src_ref=plane_sums.at[f, dest, :, :, low:high],
            dst_ref=target.at[f, dest, :, :, low:high],
            send_sem=sum_send.at[q, dest],
            recv_sem=sum_recv.at[q, dest, 0 if up else 1],
            device_id={"grp": lax.rem(z + step, nz)},
            device_id_type=MESH,
        )

    def pass_on(q, dest, up, first):
        f, low, high = grad_pieces[q]
        incoming = from_below if up else from_above
        if not first:
            sum_copy(q, dest, up).wait_recv()

            @pl.loop(0, experts)
            def _(e):
                plane_sums[f, dest, e, :, low:high] = (
                    plane_sums[f, dest, e, :, low:high].astype(f32)
                    + incoming[f, dest, e, :, low:high].astype(f32)
                ).astype(bf16)

        sum_copy(q, dest, up).start()

    def sum_turn(q, turn):
        for up in (True, False):
            dest = nz - 1 - turn if up else turn
            edge = z == 0 if up else z == nz - 1
            short = z < dest if up else z > dest

            @pl.when(short & edge)
            def _():
                pass_on(q, dest, up, True)

            @pl.when(short & jnp.logical_not(edge))
            def _():
                pass_on(q, dest, up, False)

    def sum_level(q, level):
        @pl.when(z == level)
        def _():
            for dest in range(nz - 1, level, -1):
                pass_on(q, dest, True, level == 0)

        @pl.when(z == nz - 1 - level)
        def _():
            for dest in range(nz - 1 - level):
                pass_on(q, dest, False, level == 0)

    def ret_copy(k):
        return pltpu.make_async_remote_copy(
            src_ref=ret.at[block_rows(k)],
            dst_ref=back.at[block_rows(k)],
            send_sem=ret_send.at[k],
            recv_sem=ret_recv.at[k],
            device_id={"ep": lax.rem(me + ne - k, ne)},
            device_id_type=MESH,
        )

    def first_half(f):
        x = rows[:, 0:model]
        gate = rows[:, 2 * model : 2 * model + LANES].astype(f32)
        full = weights[f, :, :, 0 : 2 * width].reshape(model, 2 * width)
        pre = jnp.dot(x, full, preferred_element_type=f32)
        a, b = pre[:, :width], pre[:, width:]
        sig = jax.nn.sigmoid(a)
        hidden_f = (a * sig * b).astype(bf16).astype(f32)
        gated = (gate * hidden_f).astype(bf16)

        @pl.loop(0, nz)
        def _(g):
            here = pl.ds(pl.multiple_of(g * shard, shard), shard)
            dn = jnp.dot(dy_t[here, :], gated, preferred_element_type=f32).astype(bf16)
            slot_grads[f, :, g, :, 2 * width :] = dn.reshape(ne, own_rows, width)

        if f == last:
            for k in range(1, ne):
                grad_copy(last, k).start()
        return a, b, sig, hidden_f

    def second_half(f, a, b, sig, hidden_f):
        dy = rows[:, model : 2 * model]
        gate = rows[:, 2 * model : 2 * model + LANES].astype(f32)
        full = weights[f, :, :, 2 * width :].reshape(model, width)
        upstream = jnp.dot(dy, full, preferred_element_type=f32)
        gate_part = upstream * hidden_f
        if f == 0:
            gate_acc[...] = gate_part
        else:
            gate_acc[...] += gate_part
        hidden_grad = gate * upstream
        da = hidden_grad * b * sig * (1.0 + a * (1.0 - sig))
        db = hidden_grad * (a * sig)
        pre_grad = jnp.concatenate([da, db], axis=1).astype(bf16)

        @pl.loop(0, nz)
        def _(g):
            here = pl.ds(pl.multiple_of(g * shard, shard), shard)
            gu = jnp.dot(x_t[here, :], pre_grad, preferred_element_type=f32).astype(bf16)
            slot_grads[f, :, g, :, 0 : 2 * width] = gu.reshape(ne, own_rows, 2 * width)

        for k in range(1, ne):
            grad_copy(f + 1 if f == last else f, k).start()

        @pl.loop(0, nz)
        def _(g):
            here = pl.ds(pl.multiple_of(g * shard, shard), shard)
            part = lax.dot_general(
                pre_grad,
                weights[f, g, :, 0 : 2 * width],
                (((1,), (1,)), ((), ())),
                preferred_element_type=f32,
            )
            if f == 0:
                row_acc[:, here] = part
            elif f < last:
                row_acc[:, here] += part
            else:
                ret[:, here] = (row_acc[:, here] + part).astype(bf16)

    def compute(f):
        second_half(f, *first_half(f))

    def grads_in(q):
        for k in range(1, ne):
            grad_copy(q, k).wait_recv()

    def plane_sum(q):
        f, low, high = grad_pieces[q]

        @pl.loop(0, nz)
        def _(g):
            @pl.loop(0, own_rows // ROW_TILE)
            def _(r):
                here = pl.ds(pl.multiple_of(r * ROW_TILE, ROW_TILE), ROW_TILE)
                total = [None] * experts
                for k in range(ne):
                    if k == 0:
                        value = slot_grads[f, me, g, here, low:high].astype(f32)
                    else:
                        value = peer_grads[f, k, g, here, low:high].astype(f32)
                    for e in range(experts):
                        term = value * mask[e][k]
                        total[e] = term if total[e] is None else total[e] + term
                for e in range(experts):
                    plane_sums[f, g, e, here, low:high] = total[e].astype(bf16)

    def finish(q):
        f, low, high = grad_pieces[q]

        def add(incoming, first):
            @pl.loop(0, experts)
            def _(e):
                value = incoming[f, z, e, :, low:high].astype(f32)
                if first:
                    value = value + plane_sums[f, z, e, :, low:high].astype(f32)
                for part in range(low // width, high // width):
                    start = part * hidden_width + f * width
                    here = value[:, part * width - low : (part + 1) * width - low] / nz
                    if first:
                        wgrad_ref[e, :, start : start + width] = here
                    else:
                        wgrad_ref[e, :, start : start + width] += here

        @pl.when(z > 0)
        def _():
            sum_copy(q, z, True).wait_recv()
            add(from_below, True)

        @pl.when((z > 0) & (z < nz - 1))
        def _():
            sum_copy(q, z, False).wait_recv()
            add(from_above, False)

        @pl.when(z == 0)
        def _():
            sum_copy(q, z, False).wait_recv()
            add(from_above, True)

    start_own(0)
    for f in range(1, chunks):
        stage(f)
    if chunks > 1:
        start_own(1)

    live = [1 - failed_ref[z, s] for s in range(ne)]
    tokens_here = tok_ref.shape[0]
    square = (tokens_here, LANES)
    lane = lax.broadcasted_iota(jnp.int32, square, 1)
    hosts_row = lax.broadcasted_iota(jnp.int32, (LANES, LANES), 0)
    hosts_lane = lax.broadcasted_iota(jnp.int32, (LANES, LANES), 1)
    hosts = jnp.zeros((LANES, LANES), f32)
    replicas = jnp.zeros(square, f32)
    ordinal = jnp.zeros(square, f32)
    for s in range(ne):
        served = live[s].astype(f32)
        hosts += jnp.where(
            (hosts_row == plan_ref[s]) & (hosts_lane == s), served, 0.0
        )
        replicas += jnp.where(lane == plan_ref[s], served, 0.0)
        before = jnp.int32(0)
        for other in range(s):
            before += (plan_ref[other] == plan_ref[s]).astype(jnp.int32) * live[other]
        ordinal += jnp.where(lane == s, before.astype(f32), 0.0)
    hosts = hosts.astype(bf16)
    earlier = (
        lax.broadcasted_iota(jnp.int32, (tokens_here, tokens_here), 1)
        < lax.broadcasted_iota(jnp.int32, (tokens_here, tokens_here), 0)
    ).astype(f32).astype(bf16)

    def column(ref, k):
        return jnp.broadcast_to(ref[k : k + 1, :], (LANES, tokens_here)).T

    wanted = [
        (lane == column(route_ref, k)).astype(f32) for k in range(2)
    ]
    ranks = jnp.dot(earlier, (wanted[0] + wanted[1]).astype(bf16), preferred_element_type=f32)
    chosen = []
    for k in range(2):
        rank = jnp.sum(wanted[k] * ranks, axis=1, keepdims=True)
        n = jnp.sum(wanted[k] * replicas, axis=1, keepdims=True)
        pick = rank - n * jnp.floor((rank + 0.5) / n)
        hosting = jnp.dot(wanted[k].astype(bf16), hosts, preferred_element_type=f32)
        chosen.append(jnp.where(jnp.abs(ordinal - pick) < 0.5, hosting, 0.0))
    places = jnp.dot(earlier, (chosen[0] + chosen[1]).astype(bf16), preferred_element_type=f32)
    offset = (lax.rem(lane - me + ne, ne) * block).astype(f32)
    spot = lax.broadcasted_iota(jnp.int32, (tokens_here, count), 1)
    gate_wide = []
    for k in range(2):
        place = jnp.sum(
            jnp.where(lane < ne, chosen[k] * (places + offset), 0.0), axis=1, keepdims=True
        )
        hot = (spot == place.astype(jnp.int32)).astype(f32)
        unpack_ref[k] = hot.astype(bf16)
        pack_ref[k] = hot.T.astype(bf16)
        gate_row = jnp.broadcast_to(gate_ref[k : k + 1, :].astype(f32), (LANES, tokens_here))
        gate_wide.append(gate_row.T.astype(bf16))
    mask = []
    for e in range(experts):
        mask.append([])
        for k in range(ne):
            slot = lax.rem(me - k + ne, ne)
            hosted = (plan_ref[slot] == e).astype(jnp.int32) * (1 - failed_ref[z, slot])
            mask[e].append(hosted.astype(f32))

    @pl.loop(1, ne)
    def _(k):
        pack(k, send_rows)
        out_copy(k).start()

    pack(0, rows)

    def rows_ready():
        for k in range(1, ne):
            out_copy(k).wait_recv()

        @pl.loop(0, model // LANES)
        def _(c):
            here = pl.ds(pl.multiple_of(c * LANES, LANES), LANES)
            there = pl.ds(pl.multiple_of(model + c * LANES, LANES), LANES)
            x_t[here, :] = rows[:, here].T
            dy_t[here, :] = rows[:, there].T

    def hop_range(f, low, high):
        for hop in range(low, min(high, nz)):
            arrive(f, hop)

    duties = []

    def work():
        if duties:
            duties.pop(0)()

    def first_level(q):
        grads_in(q)
        plane_sum(q)
        sum_level(q, 0)

    def levels(q):
        duties.append(functools.partial(first_level, q))
        for level in range(1, nz - 1):
            duties.append(functools.partial(sum_level, q, level))

    def hops_between(p):
        for hop in range(1, nz):
            arrive(p, hop)
            work()

    hop_range(0, 1, nz)
    for f in range(1, last):
        start_own(f + 1)
        if f == 1:
            hop_range(1, 1, nz - 1)
            rows_ready()
            compute(0)
            hop_range(1, nz - 1, nz)
        else:
            levels(f - 2)
            hops_between(f)
        compute(f)
    start_own(last + 1)
    levels(last - 2)
    hops_between(last)
    kept = first_half(last)
    hops_between(last + 1)
    second_half(last, *kept)
    ret[:, model : model + LANES] = jnp.broadcast_to(
        jnp.sum(gate_acc[...], axis=1, keepdims=True), (count, LANES)
    ).astype(bf16)
    while duties:
        work()
    for q in (last - 1, last):
        grads_in(q)
        plane_sum(q)
        for turn in range(nz - 1):
            sum_turn(q, turn)
    grads_in(last + 1)
    for k in range(1, ne):
        ret_copy(k).start()
    plane_sum(last + 1)
    for turn in range(nz - 1):
        sum_turn(last + 1, turn)
    for q in range(last + 1):
        finish(q)
    back[0:block, :] = ret[0:block, :]

    for k in range(1, ne):
        ret_copy(k).wait_recv()
    first, second = unpack_ref[0], unpack_ref[1]
    both = first + second

    @pl.loop(0, nz)
    def _(g):
        here = pl.ds(pl.multiple_of(g * shard, shard), shard)
        tgrad_ref[:, here] = jnp.dot(
            both, back[:, here], preferred_element_type=f32
        ).astype(bf16)

    gates_back = back[:, model : model + LANES]
    ggrad_ref[...] = jnp.where(
        lane == 0,
        jnp.dot(first, gates_back, preferred_element_type=f32),
        jnp.dot(second, gates_back, preferred_element_type=f32),
    ).astype(bf16)

    finish(last + 1)

    shard_sends_done()
    for k in range(1, ne):
        out_copy(k).wait_send()
        ret_copy(k).wait_send()
    for q in range(len(grad_pieces)):
        for k in range(1, ne):
            grad_copy(q, k).wait_send()
        for dest in range(nz):
            for up in (True, False):
                @pl.when(z < dest if up else z > dest)
                def _():
                    sum_copy(q, dest, up).wait_send()


def fused(tokens, out_grad, routes, gates, w_gate_up, w_down, plan, failed):
    nz = lax.axis_size("grp")
    ne = lax.axis_size("ep")
    tok_count, model = tokens.shape
    topk = routes.shape[1]
    experts = ne // 2
    capacity = tok_count * topk * 5 // (4 * ne)
    block = -(-capacity // ROW_TILE) * ROW_TILE
    count = ne * block
    shard = w_gate_up.shape[1]
    hidden_width = w_down.shape[2]
    width = LANES
    chunks = hidden_width // width
    own_rows = model // (nz * ne)
    bf16, f32 = jnp.bfloat16, jnp.float32
    vmem = pl.BlockSpec(memory_space=pltpu.VMEM)
    dma = pltpu.SemaphoreType.DMA
    tgrad, ggrad, wgrad = pl.pallas_call(
        functools.partial(fused_kernel, nz, ne, block),
        out_shape=(
            jax.ShapeDtypeStruct((tok_count, model), bf16),
            jax.ShapeDtypeStruct((tok_count, LANES), bf16),
            jax.ShapeDtypeStruct((experts, own_rows, 3 * hidden_width), f32),
        ),
        in_specs=[vmem] * 6 + [pl.BlockSpec(memory_space=pltpu.SMEM)] * 2,
        out_specs=(vmem, vmem, vmem),
        scratch_shapes=[
            pltpu.VMEM((chunks, nz, shard, 3 * width), bf16),
            pltpu.VMEM((count, 2 * model + LANES), bf16),
            pltpu.VMEM((count, 2 * model + LANES), bf16),
            pltpu.VMEM((model, count), bf16),
            pltpu.VMEM((model, count), bf16),
            pltpu.VMEM((count, model), f32),
            pltpu.VMEM((count, width), f32),
            pltpu.VMEM((chunks, ne, nz, own_rows, 3 * width), bf16),
            pltpu.VMEM((chunks, ne, nz, own_rows, 3 * width), bf16),
            pltpu.VMEM((chunks, nz, experts, own_rows, 3 * width), bf16),
            pltpu.VMEM((chunks, nz, experts, own_rows, 3 * width), bf16),
            pltpu.VMEM((chunks, nz, experts, own_rows, 3 * width), bf16),
            pltpu.VMEM((count, model + LANES), bf16),
            pltpu.VMEM((count, model + LANES), bf16),
            pltpu.VMEM((topk, count, tok_count), bf16),
            pltpu.VMEM((topk, tok_count, count), bf16),
            dma((chunks + 1, nz, 2)),
            dma((chunks + 1, nz)),
            dma((ne,)),
            dma((ne,)),
            dma((chunks + 1, ne)),
            dma((chunks + 1, ne)),
            dma((chunks + 1, nz)),
            dma((chunks + 1, nz, 2)),
            dma((ne,)),
            dma((ne,)),
        ],
        compiler_params=pltpu.CompilerParams(
            collective_id=0, has_side_effects=True, vmem_limit_bytes=60 * 1024 * 1024
        ),
        cost_estimate=pl.CostEstimate(
            flops=18 * count * model * hidden_width,
            bytes_accessed=16 * 1024 * 1024,
            transcendentals=count * hidden_width,
        ),
    )(tokens, out_grad, routes.T, gates.T, w_gate_up, w_down, plan, failed)
    return (tgrad, ggrad[:, :topk], wgrad)


def local(tokens, out_grad, routes, gates, w_gate_up, w_down, plan, failed):
    groups = lax.axis_size("grp")
    slot_count = lax.axis_size("ep")
    my_group = lax.axis_index("grp")
    tok_count, model_width = tokens.shape
    topk_count = routes.shape[1]
    experts = slot_count // 2
    capacity = tok_count * topk_count * 5 // (4 * slot_count)
    route_count = tok_count * topk_count
    buffer_rows = slot_count * capacity
    in_service = 1 - lax.dynamic_index_in_dim(failed, my_group, 0, keepdims=False)
    slot_index, slot_rank = assign(routes, plan, in_service, capacity, experts)
    positions = slot_index * capacity + slot_rank
    source = (
        jnp.full((buffer_rows,), route_count, jnp.int32)
        .at[positions]
        .set(jnp.arange(route_count, dtype=jnp.int32))
    )
    token_of = source // topk_count
    zero_row = jnp.zeros((1, model_width), jnp.bfloat16)
    send_x = jnp.concatenate([tokens, zero_row], axis=0)[token_of].reshape(
        slot_count, capacity, model_width
    )
    send_dy = jnp.concatenate([out_grad, zero_row], axis=0)[token_of].reshape(
        slot_count, capacity, model_width
    )
    send_gate = jnp.concatenate([gates.reshape(route_count), jnp.zeros((1,), jnp.bfloat16)])[source]
    send_gate = send_gate.reshape(slot_count, capacity)
    recv_x, recv_dy, recv_gate = (
        lax.all_to_all(send_x, "ep", split_axis=0, concat_axis=0, tiled=True),
        lax.all_to_all(send_dy, "ep", split_axis=0, concat_axis=0, tiled=True),
        lax.all_to_all(send_gate, "ep", split_axis=0, concat_axis=0, tiled=True),
    )
    full_gu, full_dn = (
        lax.all_gather(w_gate_up, "grp", axis=1, tiled=True),
        lax.all_gather(w_down, "grp", axis=1, tiled=True),
    )
    full_gu = full_gu[0]
    full_dn = full_dn[0]
    hidden_width = full_dn.shape[1]
    flat_x = recv_x.reshape(buffer_rows, model_width)
    flat_dy = recv_dy.reshape(buffer_rows, model_width)
    flat_gate = recv_gate.reshape(buffer_rows)
    row_grads, gate_rows, grad_gu, grad_dn = expert_rows(
        flat_x, flat_dy, flat_gate, full_gu, full_dn
    )
    back_x, back_gate = (
        lax.all_to_all(
            row_grads.reshape(slot_count, capacity, model_width),
            "ep",
            split_axis=0,
            concat_axis=0,
            tiled=True,
        ),
        lax.all_to_all(
            gate_rows.reshape(slot_count, capacity), "ep", split_axis=0, concat_axis=0, tiled=True
        ),
    )
    route_rows = back_x.reshape(buffer_rows, model_width)[positions]
    token_grad = jnp.sum(
        route_rows.reshape(tok_count, topk_count, model_width).astype(jnp.float32), axis=1
    ).astype(jnp.bfloat16)
    gate_grad = back_gate.reshape(buffer_rows)[positions].reshape(tok_count, topk_count)
    columns = 3 * hidden_width
    rows_each = model_width // (groups * slot_count)
    slot_grad = jnp.concatenate([grad_gu, grad_dn], axis=1).astype(jnp.bfloat16)
    slot_grad = slot_grad.reshape(groups, slot_count, rows_each, columns)
    expert_ids = jnp.arange(experts, dtype=jnp.int32)
    mixed = lax.all_to_all(
        lax.all_to_all(slot_grad, "grp", split_axis=0, concat_axis=0, tiled=True),
        "ep",
        split_axis=1,
        concat_axis=1,
        tiled=True,
    )
    hosted_all = (
        (plan[None, None, :] == expert_ids[None, :, None]) & (failed[:, None, :] == 0)
    ).astype(jnp.bfloat16)
    per_group = jnp.einsum("ges,gsrc->gerc", hosted_all, mixed, preferred_element_type=jnp.float32)
    weight_grad = jnp.sum(per_group, axis=0) / groups
    return (token_grad, gate_grad, weight_grad)


def solution(mesh):
    nz, ne = mesh.shape["grp"], mesh.shape["ep"]

    def step(tokens, *others):
        aligned = tokens.shape[1] % (nz * ne * ROW_TILE) == 0
        return (fused if aligned else local)(tokens, *others)

    placed = (
        P(("grp", "ep"), None),
        P(("grp", "ep"), None),
        P(("grp", "ep"), None),
        P(("grp", "ep"), None),
        P("ep", "grp", None),
        P("ep", "grp", None),
        P(),
        P(),
    )
    return jax.shard_map(
        step,
        mesh=mesh,
        in_specs=placed,
        out_specs=(P(("grp", "ep"), None), P(("grp", "ep"), None), P(None, ("grp", "ep"), None)),
        check_vma=False,
    )
```

```python
import functools

import jax
import jax.numpy as jnp
from jax import lax
from jax.experimental import pallas as pl
from jax.experimental.pallas import tpu as pltpu
from jax.sharding import PartitionSpec as P


def assign(route_ids, hosting, in_service, capacity, experts):
    route_count = route_ids.shape[0] * route_ids.shape[1]
    slot_count = hosting.shape[0]
    flat_routes = route_ids.reshape(route_count)
    expert_ids = jnp.arange(experts, dtype=jnp.int32)
    hosted = ((hosting[None, :] == expert_ids[:, None]) & (in_service[None, :] > 0)).astype(
        jnp.int32
    )
    replicas = jnp.sum(hosted, axis=1)
    ordinal = jnp.sum(hosted * (jnp.cumsum(hosted, axis=1) - 1), axis=0)
    expert_hot = (flat_routes[:, None] == expert_ids[None, :]).astype(jnp.int32)
    expert_rank = jnp.sum(expert_hot * (jnp.cumsum(expert_hot, axis=0) - 1), axis=1)
    route_replicas = jnp.sum(expert_hot * replicas[None, :], axis=1)
    replica_pick = expert_rank % route_replicas
    slot_hot = (
        (hosting[None, :] == flat_routes[:, None])
        & (in_service[None, :] > 0)
        & (ordinal[None, :] == replica_pick[:, None])
    ).astype(jnp.int32)
    slot_rank = jnp.sum(slot_hot * (jnp.cumsum(slot_hot, axis=0) - 1), axis=1)
    slot_index = jnp.sum(slot_hot * jnp.arange(slot_count, dtype=jnp.int32)[None, :], axis=1)
    return slot_index, slot_rank


def expert_rows(rows_x, rows_dy, rows_gate, full_gu, full_dn):
    hidden_width = full_dn.shape[1]
    projected = jnp.dot(rows_x, full_gu, preferred_element_type=jnp.float32)
    gate_pre = projected[:, :hidden_width]
    up_pre = projected[:, hidden_width:]
    sigmoid_a = jax.nn.sigmoid(gate_pre)
    silu_a = gate_pre * sigmoid_a
    hidden = (silu_a * up_pre).astype(jnp.bfloat16)
    upstream = jnp.dot(rows_dy, full_dn, preferred_element_type=jnp.float32)
    rebuilt = lax.dot_general(
        hidden, full_dn, (((1,), (1,)), ((), ())), preferred_element_type=jnp.float32
    )
    gate_grad = jnp.sum(rows_dy.astype(jnp.float32) * rebuilt, axis=1).astype(jnp.bfloat16)
    gate_value = rows_gate.astype(jnp.float32)[:, None]
    hidden_grad = gate_value * upstream
    gate_delta = hidden_grad * up_pre * sigmoid_a * (1.0 + gate_pre * (1.0 - sigmoid_a))
    up_delta = hidden_grad * silu_a
    pre_grad = jnp.concatenate([gate_delta, up_delta], axis=1).astype(jnp.bfloat16)
    row_grad = lax.dot_general(
        pre_grad, full_gu, (((1,), (1,)), ((), ())), preferred_element_type=jnp.float32
    ).astype(jnp.bfloat16)
    gated_hidden = (gate_value * hidden.astype(jnp.float32)).astype(jnp.bfloat16)
    grad_gu = lax.dot_general(
        rows_x, pre_grad, (((0,), (0,)), ((), ())), preferred_element_type=jnp.float32
    )
    grad_dn = lax.dot_general(
        rows_dy, gated_hidden, (((0,), (0,)), ((), ())), preferred_element_type=jnp.float32
    )
    return (row_grad, gate_grad, grad_gu, grad_dn)


MESH = pl.DeviceIdType.MESH
LANES = 128
ROW_TILE = 16


def fused_kernel(
    nz, ne, block,
    tok_ref, dy_ref, route_ref, gate_ref, gu_ref, dn_ref, plan_ref, failed_ref,
    tgrad_ref, ggrad_ref, wgrad_ref,
    weights, send_rows, rows, x_t, dy_t, row_acc, gate_acc, slot_grads, peer_grads,
    plane_sums, from_below, from_above, ret, back, pack_ref, unpack_ref,
    ag_send, ag_recv, out_send, out_recv, grad_send, grad_recv, sum_send, sum_recv,
    ret_send, ret_recv,
):
    z = lax.axis_index("grp")
    me = lax.axis_index("ep")
    chunks, _, shard, width3 = weights.shape
    model = nz * shard
    width = width3 // 3
    hidden_width = chunks * width
    experts = wgrad_ref.shape[0]
    own_rows = wgrad_ref.shape[1]
    count = ne * block
    f32, bf16 = jnp.float32, jnp.bfloat16
    last = chunks - 1
    both_parts, gu_part, dn_part = (0, width3), (0, 2 * width), (2 * width, width3)
    weight_pieces = [(f,) + both_parts for f in range(last)]
    weight_pieces += [(last,) + gu_part, (last,) + dn_part]
    grad_pieces = [(f,) + both_parts for f in range(last)]
    grad_pieces += [(last,) + dn_part, (last,) + gu_part]

    barrier = pltpu.get_barrier_semaphore()
    for k in range(1, ne):
        pl.semaphore_signal(
            barrier, inc=1, device_id={"ep": lax.rem(me + k, ne)}, device_id_type=MESH
        )
    for k in range(1, nz):
        pl.semaphore_signal(
            barrier, inc=1, device_id={"grp": lax.rem(z + k, nz)}, device_id_type=MESH
        )

    def stage(f):
        cols = slice(f * width, (f + 1) * width)
        up_cols = slice(hidden_width + f * width, hidden_width + (f + 1) * width)
        weights[f, z, :, 0:width] = gu_ref[0, :, cols]
        weights[f, z, :, width : 2 * width] = gu_ref[0, :, up_cols]
        weights[f, z, :, 2 * width : 3 * width] = dn_ref[0, :, cols]

    stage(0)
    pl.semaphore_wait(barrier, ne - 1 + nz - 1)

    def shard_copy(p, owner, up):
        step = 1 if up else nz - 1
        f, low, high = weight_pieces[p]
        return pltpu.make_async_remote_copy(
            src_ref=weights.at[f, owner, :, low:high],
            dst_ref=weights.at[f, owner, :, low:high],
            send_sem=ag_send.at[p, owner, 0 if up else 1],
            recv_sem=ag_recv.at[p, owner],
            device_id={"grp": lax.rem(z + step, nz)},
            device_id_type=MESH,
        )

    def start_own(p):
        @pl.when(z < nz - 1)
        def _():
            shard_copy(p, z, True).start()

        @pl.when(z > 0)
        def _():
            shard_copy(p, z, False).start()

    def arrive(p, hop):
        @pl.when(z >= hop)
        def _():
            shard_copy(p, z - hop, True).wait_recv()

            @pl.when(z < nz - 1)
            def _():
                shard_copy(p, z - hop, True).start()

        @pl.when(z + hop < nz)
        def _():
            shard_copy(p, z + hop, False).wait_recv()

            @pl.when(z > 0)
            def _():
                shard_copy(p, z + hop, False).start()

    def shard_sends_done():
        for p in range(len(weight_pieces)):
            for hop in range(nz):
                @pl.when((z >= hop) & (z < nz - 1))
                def _():
                    shard_copy(p, z - hop, True).wait_send()

                @pl.when((z + hop < nz) & (z > 0))
                def _():
                    shard_copy(p, z + hop, False).wait_send()

    def block_rows(k):
        return pl.ds(pl.multiple_of(k * block, ROW_TILE), block)

    def out_copy(k):
        return pltpu.make_async_remote_copy(
            src_ref=send_rows.at[block_rows(k)],
            dst_ref=rows.at[block_rows(k)],
            send_sem=out_send.at[k],
            recv_sem=out_recv.at[k],
            device_id={"ep": lax.rem(me + k, ne)},
            device_id_type=MESH,
        )

    def pack(k, target):
        here = block_rows(k)
        first, second = pack_ref[0, here, :], pack_ref[1, here, :]
        both = first + second
        target[here, 0:model] = jnp.dot(
            both, tok_ref[...], preferred_element_type=f32
        ).astype(bf16)
        target[here, model : 2 * model] = jnp.dot(
            both, dy_ref[...], preferred_element_type=f32
        ).astype(bf16)
        target[here, 2 * model : 2 * model + LANES] = (
            jnp.dot(first, gate_wide[0], preferred_element_type=f32)
            + jnp.dot(second, gate_wide[1], preferred_element_type=f32)
        ).astype(bf16)

    def grad_copy(q, k):
        f, low, high = grad_pieces[q]
        return pltpu.make_async_remote_copy(
            src_ref=slot_grads.at[f, lax.rem(me + k, ne), :, :, low:high],
            dst_ref=peer_grads.at[f, k, :, :, low:high],
            send_sem=grad_send.at[q, k],
            recv_sem=grad_recv.at[q, k],
            device_id={"ep": lax.rem(me + k, ne)},
            device_id_type=MESH,
        )

    def sum_copy(q, dest, up):
        step = 1 if up else nz - 1
        target = from_below if up else from_above
        f, low, high = grad_pieces[q]
        return pltpu.make_async_remote_copy(
            src_ref=plane_sums.at[f, dest, :, :, low:high],
            dst_ref=target.at[f, dest, :, :, low:high],
            send_sem=sum_send.at[q, dest],
            recv_sem=sum_recv.at[q, dest, 0 if up else 1],
            device_id={"grp": lax.rem(z + step, nz)},
            device_id_type=MESH,
        )

    def pass_on(q, dest, up, first):
        f, low, high = grad_pieces[q]
        incoming = from_below if up else from_above
        if not first:
            sum_copy(q, dest, up).wait_recv()

            @pl.loop(0, experts)
            def _(e):
                plane_sums[f, dest, e, :, low:high] = (
                    plane_sums[f, dest, e, :, low:high].astype(f32)
                    + incoming[f, dest, e, :, low:high].astype(f32)
                ).astype(bf16)

        sum_copy(q, dest, up).start()

    def sum_turn(q, turn):
        lower = 2 * z < nz

        def serve(up, allowed):
            dest = nz - 1 - turn if up else turn
            edge = z == 0 if up else z == nz - 1
            short = (z < dest if up else z > dest) & allowed

            @pl.when(short & edge)
            def _():
                pass_on(q, dest, up, True)

            @pl.when(short & jnp.logical_not(edge))
            def _():
                pass_on(q, dest, up, False)

        serve(False, jnp.logical_not(lower))
        serve(True, z >= 0)
        serve(False, lower)

    def sum_level(q, level):
        @pl.when(z == level)
        def _():
            for dest in range(nz - 1, level, -1):
                pass_on(q, dest, True, level == 0)

        @pl.when(z == nz - 1 - level)
        def _():
            for dest in range(nz - 1 - level):
                pass_on(q, dest, False, level == 0)

    def ret_copy(k):
        return pltpu.make_async_remote_copy(
            src_ref=ret.at[block_rows(k)],
            dst_ref=back.at[block_rows(k)],
            send_sem=ret_send.at[k],
            recv_sem=ret_recv.at[k],
            device_id={"ep": lax.rem(me + ne - k, ne)},
            device_id_type=MESH,
        )

    def first_half(f):
        x = rows[:, 0:model]
        gate = rows[:, 2 * model : 2 * model + LANES].astype(f32)
        full = weights[f, :, :, 0 : 2 * width].reshape(model, 2 * width)
        pre = jnp.dot(x, full, preferred_element_type=f32)
        a, b = pre[:, :width], pre[:, width:]
        sig = jax.nn.sigmoid(a)
        hidden_f = (a * sig * b).astype(bf16).astype(f32)
        gated = (gate * hidden_f).astype(bf16)

        @pl.loop(0, nz)
        def _(g):
            here = pl.ds(pl.multiple_of(g * shard, shard), shard)
            dn = jnp.dot(dy_t[here, :], gated, preferred_element_type=f32).astype(bf16)
            slot_grads[f, :, g, :, 2 * width :] = dn.reshape(ne, own_rows, width)

        if f == last:
            for k in range(1, ne):
                grad_copy(last, k).start()
        return a, b, sig, hidden_f

    def second_half(f, a, b, sig, hidden_f):
        dy = rows[:, model : 2 * model]
        gate = rows[:, 2 * model : 2 * model + LANES].astype(f32)
        full = weights[f, :, :, 2 * width :].reshape(model, width)
        upstream = jnp.dot(dy, full, preferred_element_type=f32)
        gate_part = upstream * hidden_f
        if f == 0:
            gate_acc[...] = gate_part
        else:
            gate_acc[...] += gate_part
        hidden_grad = gate * upstream
        da = hidden_grad * b * sig * (1.0 + a * (1.0 - sig))
        db = hidden_grad * (a * sig)
        pre_grad = jnp.concatenate([da, db], axis=1).astype(bf16)

        @pl.loop(0, nz)
        def _(g):
            here = pl.ds(pl.multiple_of(g * shard, shard), shard)
            gu = jnp.dot(x_t[here, :], pre_grad, preferred_element_type=f32).astype(bf16)
            slot_grads[f, :, g, :, 0 : 2 * width] = gu.reshape(ne, own_rows, 2 * width)

        for k in range(1, ne):
            grad_copy(f + 1 if f == last else f, k).start()
        return pre_grad

    def row_part(f, pre_grad):
        @pl.loop(0, nz)
        def _(g):
            here = pl.ds(pl.multiple_of(g * shard, shard), shard)
            part = lax.dot_general(
                pre_grad,
                weights[f, g, :, 0 : 2 * width],
                (((1,), (1,)), ((), ())),
                preferred_element_type=f32,
            )
            if f == 0:
                row_acc[:, here] = part
            elif f < last:
                row_acc[:, here] += part
            else:
                ret[:, here] = (row_acc[:, here] + part).astype(bf16)

    def compute(f):
        row_part(f, second_half(f, *first_half(f)))

    def grads_in(q):
        for k in range(1, ne):
            grad_copy(q, k).wait_recv()

    def plane_sum(q):
        f, low, high = grad_pieces[q]

        @pl.loop(0, nz)
        def _(g):
            @pl.loop(0, own_rows // ROW_TILE)
            def _(r):
                here = pl.ds(pl.multiple_of(r * ROW_TILE, ROW_TILE), ROW_TILE)
                total = [None] * experts
                for k in range(ne):
                    if k == 0:
                        value = slot_grads[f, me, g, here, low:high].astype(f32)
                    else:
                        value = peer_grads[f, k, g, here, low:high].astype(f32)
                    for e in range(experts):
                        term = value * mask[e][k]
                        total[e] = term if total[e] is None else total[e] + term
                for e in range(experts):
                    plane_sums[f, g, e, here, low:high] = total[e].astype(bf16)

    def finish(q):
        f, low, high = grad_pieces[q]

        def add(incoming, first):
            @pl.loop(0, experts)
            def _(e):
                value = incoming[f, z, e, :, low:high].astype(f32)
                if first:
                    value = value + plane_sums[f, z, e, :, low:high].astype(f32)
                for part in range(low // width, high // width):
                    start = part * hidden_width + f * width
                    here = value[:, part * width - low : (part + 1) * width - low] / nz
                    if first:
                        wgrad_ref[e, :, start : start + width] = here
                    else:
                        wgrad_ref[e, :, start : start + width] += here

        @pl.when(z > 0)
        def _():
            sum_copy(q, z, True).wait_recv()
            add(from_below, True)

        @pl.when((z > 0) & (z < nz - 1))
        def _():
            sum_copy(q, z, False).wait_recv()
            add(from_above, False)

        @pl.when(z == 0)
        def _():
            sum_copy(q, z, False).wait_recv()
            add(from_above, True)

    start_own(0)
    for f in range(1, chunks):
        stage(f)
    if chunks > 1:
        start_own(1)

    live = [1 - failed_ref[z, s] for s in range(ne)]
    tokens_here = tok_ref.shape[0]
    square = (tokens_here, LANES)
    lane = lax.broadcasted_iota(jnp.int32, square, 1)
    hosts_row = lax.broadcasted_iota(jnp.int32, (LANES, LANES), 0)
    hosts_lane = lax.broadcasted_iota(jnp.int32, (LANES, LANES), 1)
    hosts = jnp.zeros((LANES, LANES), f32)
    replicas = jnp.zeros(square, f32)
    ordinal = jnp.zeros(square, f32)
    for s in range(ne):
        served = live[s].astype(f32)
        hosts += jnp.where(
            (hosts_row == plan_ref[s]) & (hosts_lane == s), served, 0.0
        )
        replicas += jnp.where(lane == plan_ref[s], served, 0.0)
        before = jnp.int32(0)
        for other in range(s):
            before += (plan_ref[other] == plan_ref[s]).astype(jnp.int32) * live[other]
        ordinal += jnp.where(lane == s, before.astype(f32), 0.0)
    hosts = hosts.astype(bf16)
    earlier = (
        lax.broadcasted_iota(jnp.int32, (tokens_here, tokens_here), 1)
        < lax.broadcasted_iota(jnp.int32, (tokens_here, tokens_here), 0)
    ).astype(f32).astype(bf16)

    def column(ref, k):
        return jnp.broadcast_to(ref[k : k + 1, :], (LANES, tokens_here)).T

    wanted = [
        (lane == column(route_ref, k)).astype(f32) for k in range(2)
    ]
    ranks = jnp.dot(earlier, (wanted[0] + wanted[1]).astype(bf16), preferred_element_type=f32)
    chosen = []
    for k in range(2):
        rank = jnp.sum(wanted[k] * ranks, axis=1, keepdims=True)
        n = jnp.sum(wanted[k] * replicas, axis=1, keepdims=True)
        pick = rank - n * jnp.floor((rank + 0.5) / n)
        hosting = jnp.dot(wanted[k].astype(bf16), hosts, preferred_element_type=f32)
        chosen.append(jnp.where(jnp.abs(ordinal - pick) < 0.5, hosting, 0.0))
    places = jnp.dot(earlier, (chosen[0] + chosen[1]).astype(bf16), preferred_element_type=f32)
    offset = (lax.rem(lane - me + ne, ne) * block).astype(f32)
    spot = lax.broadcasted_iota(jnp.int32, (tokens_here, count), 1)
    gate_wide = []
    for k in range(2):
        place = jnp.sum(
            jnp.where(lane < ne, chosen[k] * (places + offset), 0.0), axis=1, keepdims=True
        )
        hot = (spot == place.astype(jnp.int32)).astype(f32)
        unpack_ref[k] = hot.astype(bf16)
        pack_ref[k] = hot.T.astype(bf16)
        gate_row = jnp.broadcast_to(gate_ref[k : k + 1, :].astype(f32), (LANES, tokens_here))
        gate_wide.append(gate_row.T.astype(bf16))
    mask = []
    for e in range(experts):
        mask.append([])
        for k in range(ne):
            slot = lax.rem(me - k + ne, ne)
            hosted = (plan_ref[slot] == e).astype(jnp.int32) * (1 - failed_ref[z, slot])
            mask[e].append(hosted.astype(f32))

    @pl.loop(1, ne)
    def _(k):
        pack(k, send_rows)
        out_copy(k).start()

    pack(0, rows)

    def rows_ready():
        for k in range(1, ne):
            out_copy(k).wait_recv()

        @pl.loop(0, model // LANES)
        def _(c):
            here = pl.ds(pl.multiple_of(c * LANES, LANES), LANES)
            there = pl.ds(pl.multiple_of(model + c * LANES, LANES), LANES)
            x_t[here, :] = rows[:, here].T
            dy_t[here, :] = rows[:, there].T

    def hop_range(f, low, high):
        for hop in range(low, min(high, nz)):
            arrive(f, hop)

    duties = []

    def work():
        if duties:
            duties.pop(0)()

    def first_level(q):
        grads_in(q)
        plane_sum(q)
        sum_level(q, 0)

    def levels(q):
        duties.append(functools.partial(first_level, q))
        for level in range(1, nz - 1):
            duties.append(functools.partial(sum_level, q, level))

    def hops_between(p):
        for hop in range(1, nz):
            arrive(p, hop)
            work()

    hop_range(0, 1, nz)
    for f in range(1, last):
        start_own(f + 1)
        if f == 1:
            hop_range(1, 1, nz - 1)
            rows_ready()
            compute(0)
            hop_range(1, nz - 1, nz)
        else:
            levels(f - 2)
            hops_between(f)
        compute(f)
    start_own(last + 1)
    levels(last - 2)
    hops_between(last)
    first_level(last - 1)
    kept = first_half(last)
    hop_range(last + 1, 1, nz)
    pre_grad = second_half(last, *kept)
    for level in range(1, nz - 2):
        sum_level(last - 1, level)
    row_part(last, pre_grad)
    ret[:, model : model + LANES] = jnp.broadcast_to(
        jnp.sum(gate_acc[...], axis=1, keepdims=True), (count, LANES)
    ).astype(bf16)
    first_level(last)
    sum_level(last - 1, nz - 2)
    for level in range(1, nz - 1):
        sum_level(last, level)
    for q in range(last - 1):
        finish(q)
    grads_in(last + 1)
    for k in range(1, ne):
        ret_copy(k).start()
    plane_sum(last + 1)
    for turn in range(nz - 1):
        sum_turn(last + 1, turn)
    for q in range(last - 1, last + 1):
        finish(q)
    back[0:block, :] = ret[0:block, :]

    for k in range(1, ne):
        ret_copy(k).wait_recv()
    first, second = unpack_ref[0], unpack_ref[1]
    both = first + second

    @pl.loop(0, nz)
    def _(g):
        here = pl.ds(pl.multiple_of(g * shard, shard), shard)
        tgrad_ref[:, here] = jnp.dot(
            both, back[:, here], preferred_element_type=f32
        ).astype(bf16)

    gates_back = back[:, model : model + LANES]
    gate_grads = jnp.where(
        lane == 0,
        jnp.dot(first, gates_back, preferred_element_type=f32),
        jnp.dot(second, gates_back, preferred_element_type=f32),
    )
    ggrad_ref[...] = gate_grads.T[0:2, :].astype(bf16)

    finish(last + 1)

    shard_sends_done()
    for k in range(1, ne):
        out_copy(k).wait_send()
        ret_copy(k).wait_send()
    for q in range(len(grad_pieces)):
        for k in range(1, ne):
            grad_copy(q, k).wait_send()
        for dest in range(nz):
            for up in (True, False):
                @pl.when(z < dest if up else z > dest)
                def _():
                    sum_copy(q, dest, up).wait_send()


def fused(tokens, out_grad, routes, gates, w_gate_up, w_down, plan, failed):
    nz = lax.axis_size("grp")
    ne = lax.axis_size("ep")
    tok_count, model = tokens.shape
    topk = routes.shape[1]
    experts = ne // 2
    capacity = tok_count * topk * 5 // (4 * ne)
    block = -(-capacity // ROW_TILE) * ROW_TILE
    count = ne * block
    shard = w_gate_up.shape[1]
    hidden_width = w_down.shape[2]
    width = LANES
    chunks = hidden_width // width
    own_rows = model // (nz * ne)
    bf16, f32 = jnp.bfloat16, jnp.float32
    vmem = pl.BlockSpec(memory_space=pltpu.VMEM)
    dma = pltpu.SemaphoreType.DMA
    tgrad, ggrad, wgrad = pl.pallas_call(
        functools.partial(fused_kernel, nz, ne, block),
        out_shape=(
            jax.ShapeDtypeStruct((tok_count, model), bf16),
            jax.ShapeDtypeStruct((topk, tok_count), bf16),
            jax.ShapeDtypeStruct((experts, own_rows, 3 * hidden_width), f32),
        ),
        in_specs=[vmem] * 6 + [pl.BlockSpec(memory_space=pltpu.SMEM)] * 2,
        out_specs=(vmem, vmem, vmem),
        scratch_shapes=[
            pltpu.VMEM((chunks, nz, shard, 3 * width), bf16),
            pltpu.VMEM((count, 2 * model + LANES), bf16),
            pltpu.VMEM((count, 2 * model + LANES), bf16),
            pltpu.VMEM((model, count), bf16),
            pltpu.VMEM((model, count), bf16),
            pltpu.VMEM((count, model), f32),
            pltpu.VMEM((count, width), f32),
            pltpu.VMEM((chunks, ne, nz, own_rows, 3 * width), bf16),
            pltpu.VMEM((chunks, ne, nz, own_rows, 3 * width), bf16),
            pltpu.VMEM((chunks, nz, experts, own_rows, 3 * width), bf16),
            pltpu.VMEM((chunks, nz, experts, own_rows, 3 * width), bf16),
            pltpu.VMEM((chunks, nz, experts, own_rows, 3 * width), bf16),
            pltpu.VMEM((count, model + LANES), bf16),
            pltpu.VMEM((count, model + LANES), bf16),
            pltpu.VMEM((topk, count, tok_count), bf16),
            pltpu.VMEM((topk, tok_count, count), bf16),
            dma((chunks + 1, nz, 2)),
            dma((chunks + 1, nz)),
            dma((ne,)),
            dma((ne,)),
            dma((chunks + 1, ne)),
            dma((chunks + 1, ne)),
            dma((chunks + 1, nz)),
            dma((chunks + 1, nz, 2)),
            dma((ne,)),
            dma((ne,)),
        ],
        compiler_params=pltpu.CompilerParams(
            collective_id=0, has_side_effects=True, vmem_limit_bytes=60 * 1024 * 1024
        ),
        cost_estimate=pl.CostEstimate(
            flops=18 * count * model * hidden_width,
            bytes_accessed=16 * 1024 * 1024,
            transcendentals=count * hidden_width,
        ),
    )(tokens, out_grad, routes.T, gates.T, w_gate_up, w_down, plan, failed)
    return (tgrad, ggrad.T, wgrad)


def local(tokens, out_grad, routes, gates, w_gate_up, w_down, plan, failed):
    groups = lax.axis_size("grp")
    slot_count = lax.axis_size("ep")
    my_group = lax.axis_index("grp")
    tok_count, model_width = tokens.shape
    topk_count = routes.shape[1]
    experts = slot_count // 2
    capacity = tok_count * topk_count * 5 // (4 * slot_count)
    route_count = tok_count * topk_count
    buffer_rows = slot_count * capacity
    in_service = 1 - lax.dynamic_index_in_dim(failed, my_group, 0, keepdims=False)
    slot_index, slot_rank = assign(routes, plan, in_service, capacity, experts)
    positions = slot_index * capacity + slot_rank
    source = (
        jnp.full((buffer_rows,), route_count, jnp.int32)
        .at[positions]
        .set(jnp.arange(route_count, dtype=jnp.int32))
    )
    token_of = source // topk_count
    zero_row = jnp.zeros((1, model_width), jnp.bfloat16)
    send_x = jnp.concatenate([tokens, zero_row], axis=0)[token_of].reshape(
        slot_count, capacity, model_width
    )
    send_dy = jnp.concatenate([out_grad, zero_row], axis=0)[token_of].reshape(
        slot_count, capacity, model_width
    )
    send_gate = jnp.concatenate([gates.reshape(route_count), jnp.zeros((1,), jnp.bfloat16)])[source]
    send_gate = send_gate.reshape(slot_count, capacity)
    recv_x, recv_dy, recv_gate = (
        lax.all_to_all(send_x, "ep", split_axis=0, concat_axis=0, tiled=True),
        lax.all_to_all(send_dy, "ep", split_axis=0, concat_axis=0, tiled=True),
        lax.all_to_all(send_gate, "ep", split_axis=0, concat_axis=0, tiled=True),
    )
    full_gu, full_dn = (
        lax.all_gather(w_gate_up, "grp", axis=1, tiled=True),
        lax.all_gather(w_down, "grp", axis=1, tiled=True),
    )
    full_gu = full_gu[0]
    full_dn = full_dn[0]
    hidden_width = full_dn.shape[1]
    flat_x = recv_x.reshape(buffer_rows, model_width)
    flat_dy = recv_dy.reshape(buffer_rows, model_width)
    flat_gate = recv_gate.reshape(buffer_rows)
    row_grads, gate_rows, grad_gu, grad_dn = expert_rows(
        flat_x, flat_dy, flat_gate, full_gu, full_dn
    )
    back_x, back_gate = (
        lax.all_to_all(
            row_grads.reshape(slot_count, capacity, model_width),
            "ep",
            split_axis=0,
            concat_axis=0,
            tiled=True,
        ),
        lax.all_to_all(
            gate_rows.reshape(slot_count, capacity), "ep", split_axis=0, concat_axis=0, tiled=True
        ),
    )
    route_rows = back_x.reshape(buffer_rows, model_width)[positions]
    token_grad = jnp.sum(
        route_rows.reshape(tok_count, topk_count, model_width).astype(jnp.float32), axis=1
    ).astype(jnp.bfloat16)
    gate_grad = back_gate.reshape(buffer_rows)[positions].reshape(tok_count, topk_count)
    columns = 3 * hidden_width
    rows_each = model_width // (groups * slot_count)
    slot_grad = jnp.concatenate([grad_gu, grad_dn], axis=1).astype(jnp.bfloat16)
    slot_grad = slot_grad.reshape(groups, slot_count, rows_each, columns)
    expert_ids = jnp.arange(experts, dtype=jnp.int32)
    mixed = lax.all_to_all(
        lax.all_to_all(slot_grad, "grp", split_axis=0, concat_axis=0, tiled=True),
        "ep",
        split_axis=1,
        concat_axis=1,
        tiled=True,
    )
    hosted_all = (
        (plan[None, None, :] == expert_ids[None, :, None]) & (failed[:, None, :] == 0)
    ).astype(jnp.bfloat16)
    per_group = jnp.einsum("ges,gsrc->gerc", hosted_all, mixed, preferred_element_type=jnp.float32)
    weight_grad = jnp.sum(per_group, axis=0) / groups
    return (token_grad, gate_grad, weight_grad)


def solution(mesh):
    nz, ne = mesh.shape["grp"], mesh.shape["ep"]

    def step(tokens, *others):
        aligned = tokens.shape[1] % (nz * ne * ROW_TILE) == 0
        return (fused if aligned else local)(tokens, *others)

    placed = (
        P(("grp", "ep"), None),
        P(("grp", "ep"), None),
        P(("grp", "ep"), None),
        P(("grp", "ep"), None),
        P("ep", "grp", None),
        P("ep", "grp", None),
        P(),
        P(),
    )
    return jax.shard_map(
        step,
        mesh=mesh,
        in_specs=placed,
        out_specs=(P(("grp", "ep"), None), P(("grp", "ep"), None), P(None, ("grp", "ep"), None)),
        check_vma=False,
    )
```

```python
import functools

import jax
import jax.numpy as jnp
from jax import lax
from jax.experimental import pallas as pl
from jax.experimental.pallas import tpu as pltpu
from jax.sharding import PartitionSpec as P


def assign(route_ids, hosting, in_service, capacity, experts):
    route_count = route_ids.shape[0] * route_ids.shape[1]
    slot_count = hosting.shape[0]
    flat_routes = route_ids.reshape(route_count)
    expert_ids = jnp.arange(experts, dtype=jnp.int32)
    hosted = ((hosting[None, :] == expert_ids[:, None]) & (in_service[None, :] > 0)).astype(
        jnp.int32
    )
    replicas = jnp.sum(hosted, axis=1)
    ordinal = jnp.sum(hosted * (jnp.cumsum(hosted, axis=1) - 1), axis=0)
    expert_hot = (flat_routes[:, None] == expert_ids[None, :]).astype(jnp.int32)
    expert_rank = jnp.sum(expert_hot * (jnp.cumsum(expert_hot, axis=0) - 1), axis=1)
    route_replicas = jnp.sum(expert_hot * replicas[None, :], axis=1)
    replica_pick = expert_rank % route_replicas
    slot_hot = (
        (hosting[None, :] == flat_routes[:, None])
        & (in_service[None, :] > 0)
        & (ordinal[None, :] == replica_pick[:, None])
    ).astype(jnp.int32)
    slot_rank = jnp.sum(slot_hot * (jnp.cumsum(slot_hot, axis=0) - 1), axis=1)
    slot_index = jnp.sum(slot_hot * jnp.arange(slot_count, dtype=jnp.int32)[None, :], axis=1)
    return slot_index, slot_rank


def expert_rows(rows_x, rows_dy, rows_gate, full_gu, full_dn):
    hidden_width = full_dn.shape[1]
    projected = jnp.dot(rows_x, full_gu, preferred_element_type=jnp.float32)
    gate_pre = projected[:, :hidden_width]
    up_pre = projected[:, hidden_width:]
    sigmoid_a = jax.nn.sigmoid(gate_pre)
    silu_a = gate_pre * sigmoid_a
    hidden = (silu_a * up_pre).astype(jnp.bfloat16)
    upstream = jnp.dot(rows_dy, full_dn, preferred_element_type=jnp.float32)
    rebuilt = lax.dot_general(
        hidden, full_dn, (((1,), (1,)), ((), ())), preferred_element_type=jnp.float32
    )
    gate_grad = jnp.sum(rows_dy.astype(jnp.float32) * rebuilt, axis=1).astype(jnp.bfloat16)
    gate_value = rows_gate.astype(jnp.float32)[:, None]
    hidden_grad = gate_value * upstream
    gate_delta = hidden_grad * up_pre * sigmoid_a * (1.0 + gate_pre * (1.0 - sigmoid_a))
    up_delta = hidden_grad * silu_a
    pre_grad = jnp.concatenate([gate_delta, up_delta], axis=1).astype(jnp.bfloat16)
    row_grad = lax.dot_general(
        pre_grad, full_gu, (((1,), (1,)), ((), ())), preferred_element_type=jnp.float32
    ).astype(jnp.bfloat16)
    gated_hidden = (gate_value * hidden.astype(jnp.float32)).astype(jnp.bfloat16)
    grad_gu = lax.dot_general(
        rows_x, pre_grad, (((0,), (0,)), ((), ())), preferred_element_type=jnp.float32
    )
    grad_dn = lax.dot_general(
        rows_dy, gated_hidden, (((0,), (0,)), ((), ())), preferred_element_type=jnp.float32
    )
    return (row_grad, gate_grad, grad_gu, grad_dn)


MESH = pl.DeviceIdType.MESH
LANES = 128
ROW_TILE = 16


def fused_kernel(
    nz, ne, block,
    tok_ref, dy_ref, route_ref, gate_ref, gu_ref, dn_ref, plan_ref, failed_ref,
    tgrad_ref, ggrad_ref, wgrad_ref,
    weights, send_rows, rows, x_t, dy_t, row_acc, gate_acc, slot_grads, peer_grads,
    plane_sums, from_below, from_above, ret, back, pack_ref, unpack_ref,
    ag_send, ag_recv, out_send, out_recv, grad_send, grad_recv, sum_send, sum_recv,
    ret_send, ret_recv,
):
    z = lax.axis_index("grp")
    me = lax.axis_index("ep")
    chunks, _, shard, width3 = weights.shape
    model = nz * shard
    width = width3 // 3
    hidden_width = chunks * width
    experts = wgrad_ref.shape[0]
    own_rows = wgrad_ref.shape[1]
    count = ne * block
    f32, bf16 = jnp.float32, jnp.bfloat16
    last = chunks - 1
    both_parts, gu_part, dn_part = (0, width3), (0, 2 * width), (2 * width, width3)
    weight_pieces = [(f,) + both_parts for f in range(last)]
    weight_pieces += [(last,) + gu_part, (last,) + dn_part]
    grad_pieces = [(f,) + both_parts for f in range(last)]
    grad_pieces += [(last,) + dn_part, (last,) + gu_part]

    barrier = pltpu.get_barrier_semaphore()
    for k in range(1, ne):
        pl.semaphore_signal(
            barrier, inc=1, device_id={"ep": lax.rem(me + k, ne)}, device_id_type=MESH
        )
    for k in range(1, nz):
        pl.semaphore_signal(
            barrier, inc=1, device_id={"grp": lax.rem(z + k, nz)}, device_id_type=MESH
        )

    def stage(f):
        cols = slice(f * width, (f + 1) * width)
        up_cols = slice(hidden_width + f * width, hidden_width + (f + 1) * width)
        weights[f, z, :, 0:width] = gu_ref[0, :, cols]
        weights[f, z, :, width : 2 * width] = gu_ref[0, :, up_cols]
        weights[f, z, :, 2 * width : 3 * width] = dn_ref[0, :, cols]

    stage(0)
    pl.semaphore_wait(barrier, ne - 1 + nz - 1)

    def shard_copy(p, owner, up):
        step = 1 if up else nz - 1
        f, low, high = weight_pieces[p]
        return pltpu.make_async_remote_copy(
            src_ref=weights.at[f, owner, :, low:high],
            dst_ref=weights.at[f, owner, :, low:high],
            send_sem=ag_send.at[p, owner, 0 if up else 1],
            recv_sem=ag_recv.at[p, owner],
            device_id={"grp": lax.rem(z + step, nz)},
            device_id_type=MESH,
        )

    def start_own(p):
        @pl.when(z < nz - 1)
        def _():
            shard_copy(p, z, True).start()

        @pl.when(z > 0)
        def _():
            shard_copy(p, z, False).start()

    def arrive(p, hop):
        @pl.when(z >= hop)
        def _():
            shard_copy(p, z - hop, True).wait_recv()

            @pl.when(z < nz - 1)
            def _():
                shard_copy(p, z - hop, True).start()

        @pl.when(z + hop < nz)
        def _():
            shard_copy(p, z + hop, False).wait_recv()

            @pl.when(z > 0)
            def _():
                shard_copy(p, z + hop, False).start()

    def shard_sends_done():
        for p in range(len(weight_pieces)):
            for hop in range(nz):
                @pl.when((z >= hop) & (z < nz - 1))
                def _():
                    shard_copy(p, z - hop, True).wait_send()

                @pl.when((z + hop < nz) & (z > 0))
                def _():
                    shard_copy(p, z + hop, False).wait_send()

    def block_rows(k):
        return pl.ds(pl.multiple_of(k * block, ROW_TILE), block)

    def out_copy(k):
        return pltpu.make_async_remote_copy(
            src_ref=send_rows.at[block_rows(k)],
            dst_ref=rows.at[block_rows(k)],
            send_sem=out_send.at[k],
            recv_sem=out_recv.at[k],
            device_id={"ep": lax.rem(me + k, ne)},
            device_id_type=MESH,
        )

    def pack(k, target):
        here = block_rows(k)
        first, second = pack_ref[0, here, :], pack_ref[1, here, :]
        both = first + second
        target[here, 0:model] = jnp.dot(
            both, tok_ref[...], preferred_element_type=f32
        ).astype(bf16)
        target[here, model : 2 * model] = jnp.dot(
            both, dy_ref[...], preferred_element_type=f32
        ).astype(bf16)
        target[here, 2 * model : 2 * model + LANES] = (
            jnp.dot(first, gate_wide[0], preferred_element_type=f32)
            + jnp.dot(second, gate_wide[1], preferred_element_type=f32)
        ).astype(bf16)

    def grad_copy(q, k):
        f, low, high = grad_pieces[q]
        return pltpu.make_async_remote_copy(
            src_ref=slot_grads.at[f, lax.rem(me + k, ne), :, :, low:high],
            dst_ref=peer_grads.at[f, k, :, :, low:high],
            send_sem=grad_send.at[q, k],
            recv_sem=grad_recv.at[q, k],
            device_id={"ep": lax.rem(me + k, ne)},
            device_id_type=MESH,
        )

    def sum_copy(q, dest, up):
        step = 1 if up else nz - 1
        target = from_below if up else from_above
        f, low, high = grad_pieces[q]
        return pltpu.make_async_remote_copy(
            src_ref=plane_sums.at[f, dest, :, :, low:high],
            dst_ref=target.at[f, dest, :, :, low:high],
            send_sem=sum_send.at[q, dest],
            recv_sem=sum_recv.at[q, dest, 0 if up else 1],
            device_id={"grp": lax.rem(z + step, nz)},
            device_id_type=MESH,
        )

    def pass_on(q, dest, up, first):
        f, low, high = grad_pieces[q]
        incoming = from_below if up else from_above
        if not first:
            sum_copy(q, dest, up).wait_recv()

            @pl.loop(0, experts)
            def _(e):
                plane_sums[f, dest, e, :, low:high] = (
                    plane_sums[f, dest, e, :, low:high].astype(f32)
                    + incoming[f, dest, e, :, low:high].astype(f32)
                ).astype(bf16)

        sum_copy(q, dest, up).start()

    def sum_turn(q, turn):
        lower = 2 * z < nz

        def serve(up, allowed):
            dest = nz - 1 - turn if up else turn
            edge = z == 0 if up else z == nz - 1
            short = (z < dest if up else z > dest) & allowed

            @pl.when(short & edge)
            def _():
                pass_on(q, dest, up, True)

            @pl.when(short & jnp.logical_not(edge))
            def _():
                pass_on(q, dest, up, False)

        serve(False, jnp.logical_not(lower))
        serve(True, z >= 0)
        serve(False, lower)

    def sum_level(q, level):
        @pl.when(z == level)
        def _():
            for dest in range(nz - 1, level, -1):
                pass_on(q, dest, True, level == 0)

        @pl.when(z == nz - 1 - level)
        def _():
            for dest in range(nz - 1 - level):
                pass_on(q, dest, False, level == 0)

    def ret_copy(k):
        return pltpu.make_async_remote_copy(
            src_ref=ret.at[block_rows(k)],
            dst_ref=back.at[block_rows(k)],
            send_sem=ret_send.at[k],
            recv_sem=ret_recv.at[k],
            device_id={"ep": lax.rem(me + ne - k, ne)},
            device_id_type=MESH,
        )

    def first_half(f):
        x = rows[:, 0:model]
        gate = rows[:, 2 * model : 2 * model + LANES].astype(f32)
        full = weights[f, :, :, 0 : 2 * width].reshape(model, 2 * width)
        pre = jnp.dot(x, full, preferred_element_type=f32)
        a, b = pre[:, :width], pre[:, width:]
        sig = jax.nn.sigmoid(a)
        hidden_f = (a * sig * b).astype(bf16).astype(f32)
        gated = (gate * hidden_f).astype(bf16)

        @pl.loop(0, nz)
        def _(g):
            here = pl.ds(pl.multiple_of(g * shard, shard), shard)
            dn = jnp.dot(dy_t[here, :], gated, preferred_element_type=f32).astype(bf16)
            slot_grads[f, :, g, :, 2 * width :] = dn.reshape(ne, own_rows, width)

        if f == last:
            for k in range(1, ne):
                grad_copy(last, k).start()
        return a, b, sig, hidden_f

    def second_half(f, a, b, sig, hidden_f):
        dy = rows[:, model : 2 * model]
        gate = rows[:, 2 * model : 2 * model + LANES].astype(f32)
        full = weights[f, :, :, 2 * width :].reshape(model, width)
        upstream = jnp.dot(dy, full, preferred_element_type=f32)
        gate_part = upstream * hidden_f
        if f == 0:
            gate_acc[...] = gate_part
        else:
            gate_acc[...] += gate_part
        hidden_grad = gate * upstream
        da = hidden_grad * b * sig * (1.0 + a * (1.0 - sig))
        db = hidden_grad * (a * sig)
        pre_grad = jnp.concatenate([da, db], axis=1).astype(bf16)

        @pl.loop(0, nz)
        def _(g):
            here = pl.ds(pl.multiple_of(g * shard, shard), shard)
            gu = jnp.dot(x_t[here, :], pre_grad, preferred_element_type=f32).astype(bf16)
            slot_grads[f, :, g, :, 0 : 2 * width] = gu.reshape(ne, own_rows, 2 * width)

        for k in range(1, ne):
            grad_copy(f + 1 if f == last else f, k).start()
        return pre_grad

    def row_part(f, pre_grad):
        @pl.loop(0, nz)
        def _(g):
            here = pl.ds(pl.multiple_of(g * shard, shard), shard)
            part = lax.dot_general(
                pre_grad,
                weights[f, g, :, 0 : 2 * width],
                (((1,), (1,)), ((), ())),
                preferred_element_type=f32,
            )
            if f == 0:
                row_acc[:, here] = part
            elif f < last:
                row_acc[:, here] += part
            else:
                ret[:, here] = (row_acc[:, here] + part).astype(bf16)

    def compute(f):
        row_part(f, second_half(f, *first_half(f)))

    def grads_in(q, low=1, high=ne):
        for k in range(low, high):
            grad_copy(q, k).wait_recv()

    def plane_sum(q):
        f, low, high = grad_pieces[q]

        @pl.loop(0, nz)
        def _(g):
            @pl.loop(0, own_rows // ROW_TILE)
            def _(r):
                here = pl.ds(pl.multiple_of(r * ROW_TILE, ROW_TILE), ROW_TILE)
                total = [None] * experts
                for k in range(ne):
                    if k == 0:
                        value = slot_grads[f, me, g, here, low:high].astype(f32)
                    else:
                        value = peer_grads[f, k, g, here, low:high].astype(f32)
                    for e in range(experts):
                        term = value * mask[e][k]
                        total[e] = term if total[e] is None else total[e] + term
                for e in range(experts):
                    plane_sums[f, g, e, here, low:high] = total[e].astype(bf16)

    def finish(q):
        f, low, high = grad_pieces[q]

        def add(incoming, first):
            @pl.loop(0, experts)
            def _(e):
                value = incoming[f, z, e, :, low:high].astype(f32)
                if first:
                    value = value + plane_sums[f, z, e, :, low:high].astype(f32)
                for part in range(low // width, high // width):
                    start = part * hidden_width + f * width
                    here = value[:, part * width - low : (part + 1) * width - low] / nz
                    if first:
                        wgrad_ref[e, :, start : start + width] = here
                    else:
                        wgrad_ref[e, :, start : start + width] += here

        @pl.when(z > 0)
        def _():
            sum_copy(q, z, True).wait_recv()
            add(from_below, True)

        @pl.when((z > 0) & (z < nz - 1))
        def _():
            sum_copy(q, z, False).wait_recv()
            add(from_above, False)

        @pl.when(z == 0)
        def _():
            sum_copy(q, z, False).wait_recv()
            add(from_above, True)

    start_own(0)
    for f in range(1, chunks):
        stage(f)
    if chunks > 1:
        start_own(1)

    live = [1 - failed_ref[z, s] for s in range(ne)]
    tokens_here = tok_ref.shape[0]
    square = (tokens_here, LANES)
    lane = lax.broadcasted_iota(jnp.int32, square, 1)
    hosts_row = lax.broadcasted_iota(jnp.int32, (LANES, LANES), 0)
    hosts_lane = lax.broadcasted_iota(jnp.int32, (LANES, LANES), 1)
    hosts = jnp.zeros((LANES, LANES), f32)
    replicas = jnp.zeros(square, f32)
    ordinal = jnp.zeros(square, f32)
    for s in range(ne):
        served = live[s].astype(f32)
        hosts += jnp.where(
            (hosts_row == plan_ref[s]) & (hosts_lane == s), served, 0.0
        )
        replicas += jnp.where(lane == plan_ref[s], served, 0.0)
        before = jnp.int32(0)
        for other in range(s):
            before += (plan_ref[other] == plan_ref[s]).astype(jnp.int32) * live[other]
        ordinal += jnp.where(lane == s, before.astype(f32), 0.0)
    hosts = hosts.astype(bf16)
    earlier = (
        lax.broadcasted_iota(jnp.int32, (tokens_here, tokens_here), 1)
        < lax.broadcasted_iota(jnp.int32, (tokens_here, tokens_here), 0)
    ).astype(f32).astype(bf16)

    def column(ref, k):
        return jnp.broadcast_to(ref[k : k + 1, :], (LANES, tokens_here)).T

    wanted = [
        (lane == column(route_ref, k)).astype(f32) for k in range(2)
    ]
    ranks = jnp.dot(earlier, (wanted[0] + wanted[1]).astype(bf16), preferred_element_type=f32)
    chosen = []
    for k in range(2):
        rank = jnp.sum(wanted[k] * ranks, axis=1, keepdims=True)
        n = jnp.sum(wanted[k] * replicas, axis=1, keepdims=True)
        pick = rank - n * jnp.floor((rank + 0.5) / n)
        hosting = jnp.dot(wanted[k].astype(bf16), hosts, preferred_element_type=f32)
        chosen.append(jnp.where(jnp.abs(ordinal - pick) < 0.5, hosting, 0.0))
    places = jnp.dot(earlier, (chosen[0] + chosen[1]).astype(bf16), preferred_element_type=f32)
    offset = (lax.rem(lane - me + ne, ne) * block).astype(f32)
    spot = lax.broadcasted_iota(jnp.int32, (tokens_here, count), 1)
    gate_wide = []
    for k in range(2):
        place = jnp.sum(
            jnp.where(lane < ne, chosen[k] * (places + offset), 0.0), axis=1, keepdims=True
        )
        hot = (spot == place.astype(jnp.int32)).astype(f32)
        unpack_ref[k] = hot.astype(bf16)
        pack_ref[k] = hot.T.astype(bf16)
        gate_row = jnp.broadcast_to(gate_ref[k : k + 1, :].astype(f32), (LANES, tokens_here))
        gate_wide.append(gate_row.T.astype(bf16))
    mask = []
    for e in range(experts):
        mask.append([])
        for k in range(ne):
            slot = lax.rem(me - k + ne, ne)
            hosted = (plan_ref[slot] == e).astype(jnp.int32) * (1 - failed_ref[z, slot])
            mask[e].append(hosted.astype(f32))

    @pl.loop(1, ne)
    def _(k):
        pack(k, send_rows)
        out_copy(k).start()

    pack(0, rows)

    def rows_ready():
        for k in range(1, ne):
            out_copy(k).wait_recv()

        @pl.loop(0, model // LANES)
        def _(c):
            here = pl.ds(pl.multiple_of(c * LANES, LANES), LANES)
            there = pl.ds(pl.multiple_of(model + c * LANES, LANES), LANES)
            x_t[here, :] = rows[:, here].T
            dy_t[here, :] = rows[:, there].T

    def hop_range(f, low, high):
        for hop in range(low, min(high, nz)):
            arrive(f, hop)

    duties = []

    def work():
        if duties:
            duties.pop(0)()

    def first_level(q):
        grads_in(q)
        plane_sum(q)
        sum_level(q, 0)

    def levels(q):
        duties.append(functools.partial(first_level, q))
        for level in range(1, nz - 2):
            duties.append(functools.partial(sum_level, q, level))

    def hops_between(p):
        for hop in range(1, nz):
            arrive(p, hop)
            work()

    hop_range(0, 1, nz)
    for f in range(1, last):
        start_own(f + 1)
        if f == 1:
            hop_range(1, 1, nz - 1)
            rows_ready()
            compute(0)
            hop_range(1, nz - 1, nz)
        else:
            levels(f - 2)
            hops_between(f)
        compute(f)
    start_own(last + 1)
    levels(last - 2)
    hops_between(last)
    first_level(last - 1)
    kept = first_half(last)
    hop_range(last + 1, 1, nz)
    pre_grad = second_half(last, *kept)
    for q in range(last - 1):
        sum_level(q, nz - 2)
    for level in range(1, nz - 2):
        sum_level(last - 1, level)
    row_part(last, pre_grad)
    ret[:, model : model + LANES] = jnp.broadcast_to(
        jnp.sum(gate_acc[...], axis=1, keepdims=True), (count, LANES)
    ).astype(bf16)
    first_level(last)
    early = ne // 2
    grads_in(last + 1, 1, early)
    for k in range(1, early):
        ret_copy(k).start()
    grads_in(last + 1, early, ne)
    for k in range(early, ne):
        ret_copy(k).start()
    plane_sum(last + 1)
    sum_level(last - 1, nz - 2)
    for level in range(1, nz - 1):
        sum_level(last, level)
    for turn in range(nz - 1):
        sum_turn(last + 1, turn)
    for q in range(last + 1):
        finish(q)
    back[0:block, :] = ret[0:block, :]

    for k in range(1, ne):
        ret_copy(k).wait_recv()
    first, second = unpack_ref[0], unpack_ref[1]
    both = first + second

    @pl.loop(0, nz)
    def _(g):
        here = pl.ds(pl.multiple_of(g * shard, shard), shard)
        tgrad_ref[:, here] = jnp.dot(
            both, back[:, here], preferred_element_type=f32
        ).astype(bf16)

    gates_back = back[:, model : model + LANES]
    gate_grads = jnp.where(
        lane == 0,
        jnp.dot(first, gates_back, preferred_element_type=f32),
        jnp.dot(second, gates_back, preferred_element_type=f32),
    )
    ggrad_ref[...] = gate_grads.T[0:2, :].astype(bf16)

    finish(last + 1)

    shard_sends_done()
    for k in range(1, ne):
        out_copy(k).wait_send()
        ret_copy(k).wait_send()
    for q in range(len(grad_pieces)):
        for k in range(1, ne):
            grad_copy(q, k).wait_send()
        for dest in range(nz):
            for up in (True, False):
                @pl.when(z < dest if up else z > dest)
                def _():
                    sum_copy(q, dest, up).wait_send()


def fused(tokens, out_grad, routes, gates, w_gate_up, w_down, plan, failed):
    nz = lax.axis_size("grp")
    ne = lax.axis_size("ep")
    tok_count, model = tokens.shape
    topk = routes.shape[1]
    experts = ne // 2
    capacity = tok_count * topk * 5 // (4 * ne)
    block = -(-capacity // ROW_TILE) * ROW_TILE
    count = ne * block
    shard = w_gate_up.shape[1]
    hidden_width = w_down.shape[2]
    width = LANES
    chunks = hidden_width // width
    own_rows = model // (nz * ne)
    bf16, f32 = jnp.bfloat16, jnp.float32
    vmem = pl.BlockSpec(memory_space=pltpu.VMEM)
    dma = pltpu.SemaphoreType.DMA
    tgrad, ggrad, wgrad = pl.pallas_call(
        functools.partial(fused_kernel, nz, ne, block),
        out_shape=(
            jax.ShapeDtypeStruct((tok_count, model), bf16),
            jax.ShapeDtypeStruct((topk, tok_count), bf16),
            jax.ShapeDtypeStruct((experts, own_rows, 3 * hidden_width), f32),
        ),
        in_specs=[vmem] * 6 + [pl.BlockSpec(memory_space=pltpu.SMEM)] * 2,
        out_specs=(vmem, vmem, vmem),
        scratch_shapes=[
            pltpu.VMEM((chunks, nz, shard, 3 * width), bf16),
            pltpu.VMEM((count, 2 * model + LANES), bf16),
            pltpu.VMEM((count, 2 * model + LANES), bf16),
            pltpu.VMEM((model, count), bf16),
            pltpu.VMEM((model, count), bf16),
            pltpu.VMEM((count, model), f32),
            pltpu.VMEM((count, width), f32),
            pltpu.VMEM((chunks, ne, nz, own_rows, 3 * width), bf16),
            pltpu.VMEM((chunks, ne, nz, own_rows, 3 * width), bf16),
            pltpu.VMEM((chunks, nz, experts, own_rows, 3 * width), bf16),
            pltpu.VMEM((chunks, nz, experts, own_rows, 3 * width), bf16),
            pltpu.VMEM((chunks, nz, experts, own_rows, 3 * width), bf16),
            pltpu.VMEM((count, model + LANES), bf16),
            pltpu.VMEM((count, model + LANES), bf16),
            pltpu.VMEM((topk, count, tok_count), bf16),
            pltpu.VMEM((topk, tok_count, count), bf16),
            dma((chunks + 1, nz, 2)),
            dma((chunks + 1, nz)),
            dma((ne,)),
            dma((ne,)),
            dma((chunks + 1, ne)),
            dma((chunks + 1, ne)),
            dma((chunks + 1, nz)),
            dma((chunks + 1, nz, 2)),
            dma((ne,)),
            dma((ne,)),
        ],
        compiler_params=pltpu.CompilerParams(
            collective_id=0, has_side_effects=True, vmem_limit_bytes=60 * 1024 * 1024
        ),
        cost_estimate=pl.CostEstimate(
            flops=18 * count * model * hidden_width,
            bytes_accessed=16 * 1024 * 1024,
            transcendentals=count * hidden_width,
        ),
    )(tokens, out_grad, routes.T, gates.T, w_gate_up, w_down, plan, failed)
    return (tgrad, ggrad.T, wgrad)


def local(tokens, out_grad, routes, gates, w_gate_up, w_down, plan, failed):
    groups = lax.axis_size("grp")
    slot_count = lax.axis_size("ep")
    my_group = lax.axis_index("grp")
    tok_count, model_width = tokens.shape
    topk_count = routes.shape[1]
    experts = slot_count // 2
    capacity = tok_count * topk_count * 5 // (4 * slot_count)
    route_count = tok_count * topk_count
    buffer_rows = slot_count * capacity
    in_service = 1 - lax.dynamic_index_in_dim(failed, my_group, 0, keepdims=False)
    slot_index, slot_rank = assign(routes, plan, in_service, capacity, experts)
    positions = slot_index * capacity + slot_rank
    source = (
        jnp.full((buffer_rows,), route_count, jnp.int32)
        .at[positions]
        .set(jnp.arange(route_count, dtype=jnp.int32))
    )
    token_of = source // topk_count
    zero_row = jnp.zeros((1, model_width), jnp.bfloat16)
    send_x = jnp.concatenate([tokens, zero_row], axis=0)[token_of].reshape(
        slot_count, capacity, model_width
    )
    send_dy = jnp.concatenate([out_grad, zero_row], axis=0)[token_of].reshape(
        slot_count, capacity, model_width
    )
    send_gate = jnp.concatenate([gates.reshape(route_count), jnp.zeros((1,), jnp.bfloat16)])[source]
    send_gate = send_gate.reshape(slot_count, capacity)
    recv_x, recv_dy, recv_gate = (
        lax.all_to_all(send_x, "ep", split_axis=0, concat_axis=0, tiled=True),
        lax.all_to_all(send_dy, "ep", split_axis=0, concat_axis=0, tiled=True),
        lax.all_to_all(send_gate, "ep", split_axis=0, concat_axis=0, tiled=True),
    )
    full_gu, full_dn = (
        lax.all_gather(w_gate_up, "grp", axis=1, tiled=True),
        lax.all_gather(w_down, "grp", axis=1, tiled=True),
    )
    full_gu = full_gu[0]
    full_dn = full_dn[0]
    hidden_width = full_dn.shape[1]
    flat_x = recv_x.reshape(buffer_rows, model_width)
    flat_dy = recv_dy.reshape(buffer_rows, model_width)
    flat_gate = recv_gate.reshape(buffer_rows)
    row_grads, gate_rows, grad_gu, grad_dn = expert_rows(
        flat_x, flat_dy, flat_gate, full_gu, full_dn
    )
    back_x, back_gate = (
        lax.all_to_all(
            row_grads.reshape(slot_count, capacity, model_width),
            "ep",
            split_axis=0,
            concat_axis=0,
            tiled=True,
        ),
        lax.all_to_all(
            gate_rows.reshape(slot_count, capacity), "ep", split_axis=0, concat_axis=0, tiled=True
        ),
    )
    route_rows = back_x.reshape(buffer_rows, model_width)[positions]
    token_grad = jnp.sum(
        route_rows.reshape(tok_count, topk_count, model_width).astype(jnp.float32), axis=1
    ).astype(jnp.bfloat16)
    gate_grad = back_gate.reshape(buffer_rows)[positions].reshape(tok_count, topk_count)
    columns = 3 * hidden_width
    rows_each = model_width // (groups * slot_count)
    slot_grad = jnp.concatenate([grad_gu, grad_dn], axis=1).astype(jnp.bfloat16)
    slot_grad = slot_grad.reshape(groups, slot_count, rows_each, columns)
    expert_ids = jnp.arange(experts, dtype=jnp.int32)
    mixed = lax.all_to_all(
        lax.all_to_all(slot_grad, "grp", split_axis=0, concat_axis=0, tiled=True),
        "ep",
        split_axis=1,
        concat_axis=1,
        tiled=True,
    )
    hosted_all = (
        (plan[None, None, :] == expert_ids[None, :, None]) & (failed[:, None, :] == 0)
    ).astype(jnp.bfloat16)
    per_group = jnp.einsum("ges,gsrc->gerc", hosted_all, mixed, preferred_element_type=jnp.float32)
    weight_grad = jnp.sum(per_group, axis=0) / groups
    return (token_grad, gate_grad, weight_grad)


def solution(mesh):
    nz, ne = mesh.shape["grp"], mesh.shape["ep"]

    def step(tokens, *others):
        aligned = tokens.shape[1] % (nz * ne * ROW_TILE) == 0
        return (fused if aligned else local)(tokens, *others)

    placed = (
        P(("grp", "ep"), None),
        P(("grp", "ep"), None),
        P(("grp", "ep"), None),
        P(("grp", "ep"), None),
        P("ep", "grp", None),
        P("ep", "grp", None),
        P(),
        P(),
    )
    return jax.shard_map(
        step,
        mesh=mesh,
        in_specs=placed,
        out_specs=(P(("grp", "ep"), None), P(("grp", "ep"), None), P(None, ("grp", "ep"), None)),
        check_vma=False,
    )
```

```python
import functools

import jax
import jax.numpy as jnp
from jax import lax
from jax.experimental import pallas as pl
from jax.experimental.pallas import tpu as pltpu
from jax.sharding import PartitionSpec as P


def assign(route_ids, hosting, in_service, capacity, experts):
    route_count = route_ids.shape[0] * route_ids.shape[1]
    slot_count = hosting.shape[0]
    flat_routes = route_ids.reshape(route_count)
    expert_ids = jnp.arange(experts, dtype=jnp.int32)
    hosted = ((hosting[None, :] == expert_ids[:, None]) & (in_service[None, :] > 0)).astype(
        jnp.int32
    )
    replicas = jnp.sum(hosted, axis=1)
    ordinal = jnp.sum(hosted * (jnp.cumsum(hosted, axis=1) - 1), axis=0)
    expert_hot = (flat_routes[:, None] == expert_ids[None, :]).astype(jnp.int32)
    expert_rank = jnp.sum(expert_hot * (jnp.cumsum(expert_hot, axis=0) - 1), axis=1)
    route_replicas = jnp.sum(expert_hot * replicas[None, :], axis=1)
    replica_pick = expert_rank % route_replicas
    slot_hot = (
        (hosting[None, :] == flat_routes[:, None])
        & (in_service[None, :] > 0)
        & (ordinal[None, :] == replica_pick[:, None])
    ).astype(jnp.int32)
    slot_rank = jnp.sum(slot_hot * (jnp.cumsum(slot_hot, axis=0) - 1), axis=1)
    slot_index = jnp.sum(slot_hot * jnp.arange(slot_count, dtype=jnp.int32)[None, :], axis=1)
    return slot_index, slot_rank


def expert_rows(rows_x, rows_dy, rows_gate, full_gu, full_dn):
    hidden_width = full_dn.shape[1]
    projected = jnp.dot(rows_x, full_gu, preferred_element_type=jnp.float32)
    gate_pre = projected[:, :hidden_width]
    up_pre = projected[:, hidden_width:]
    sigmoid_a = jax.nn.sigmoid(gate_pre)
    silu_a = gate_pre * sigmoid_a
    hidden = (silu_a * up_pre).astype(jnp.bfloat16)
    upstream = jnp.dot(rows_dy, full_dn, preferred_element_type=jnp.float32)
    rebuilt = lax.dot_general(
        hidden, full_dn, (((1,), (1,)), ((), ())), preferred_element_type=jnp.float32
    )
    gate_grad = jnp.sum(rows_dy.astype(jnp.float32) * rebuilt, axis=1).astype(jnp.bfloat16)
    gate_value = rows_gate.astype(jnp.float32)[:, None]
    hidden_grad = gate_value * upstream
    gate_delta = hidden_grad * up_pre * sigmoid_a * (1.0 + gate_pre * (1.0 - sigmoid_a))
    up_delta = hidden_grad * silu_a
    pre_grad = jnp.concatenate([gate_delta, up_delta], axis=1).astype(jnp.bfloat16)
    row_grad = lax.dot_general(
        pre_grad, full_gu, (((1,), (1,)), ((), ())), preferred_element_type=jnp.float32
    ).astype(jnp.bfloat16)
    gated_hidden = (gate_value * hidden.astype(jnp.float32)).astype(jnp.bfloat16)
    grad_gu = lax.dot_general(
        rows_x, pre_grad, (((0,), (0,)), ((), ())), preferred_element_type=jnp.float32
    )
    grad_dn = lax.dot_general(
        rows_dy, gated_hidden, (((0,), (0,)), ((), ())), preferred_element_type=jnp.float32
    )
    return (row_grad, gate_grad, grad_gu, grad_dn)


MESH = pl.DeviceIdType.MESH
LANES = 128
ROW_TILE = 16


def fused_kernel(
    nz, ne, block,
    tok_ref, dy_ref, route_ref, gate_ref, gu_ref, dn_ref, plan_ref, failed_ref,
    tgrad_ref, ggrad_ref, wgrad_ref,
    weights, send_rows, rows, x_t, dy_t, row_acc, gate_acc, slot_grads, peer_grads,
    plane_sums, from_below, from_above, ret, back, pack_ref, unpack_ref,
    ag_send, ag_recv, out_send, out_recv, grad_send, grad_recv, sum_send, sum_recv,
    ret_send, ret_recv,
):
    z = lax.axis_index("grp")
    me = lax.axis_index("ep")
    chunks, _, shard, width3 = weights.shape
    model = nz * shard
    width = width3 // 3
    hidden_width = chunks * width
    experts = wgrad_ref.shape[0]
    own_rows = wgrad_ref.shape[1]
    count = ne * block
    f32, bf16 = jnp.float32, jnp.bfloat16
    last = chunks - 1
    both_parts, gu_part, dn_part = (0, width3), (0, 2 * width), (2 * width, width3)
    weight_pieces = [(f,) + both_parts for f in range(last)]
    weight_pieces += [(last,) + gu_part, (last,) + dn_part]
    grad_pieces = [(f,) + both_parts for f in range(last)]
    grad_pieces += [(last,) + dn_part, (last,) + gu_part]

    barrier = pltpu.get_barrier_semaphore()
    for k in range(1, ne):
        pl.semaphore_signal(
            barrier, inc=1, device_id={"ep": lax.rem(me + k, ne)}, device_id_type=MESH
        )
    for k in range(1, nz):
        pl.semaphore_signal(
            barrier, inc=1, device_id={"grp": lax.rem(z + k, nz)}, device_id_type=MESH
        )

    def stage(f):
        cols = slice(f * width, (f + 1) * width)
        up_cols = slice(hidden_width + f * width, hidden_width + (f + 1) * width)
        weights[f, z, :, 0:width] = gu_ref[0, :, cols]
        weights[f, z, :, width : 2 * width] = gu_ref[0, :, up_cols]
        weights[f, z, :, 2 * width : 3 * width] = dn_ref[0, :, cols]

    stage(0)
    pl.semaphore_wait(barrier, ne - 1 + nz - 1)

    def shard_copy(p, owner, up):
        step = 1 if up else nz - 1
        f, low, high = weight_pieces[p]
        return pltpu.make_async_remote_copy(
            src_ref=weights.at[f, owner, :, low:high],
            dst_ref=weights.at[f, owner, :, low:high],
            send_sem=ag_send.at[p, owner, 0 if up else 1],
            recv_sem=ag_recv.at[p, owner],
            device_id={"grp": lax.rem(z + step, nz)},
            device_id_type=MESH,
        )

    def start_own(p):
        @pl.when(z < nz - 1)
        def _():
            shard_copy(p, z, True).start()

        @pl.when(z > 0)
        def _():
            shard_copy(p, z, False).start()

    def arrive(p, hop):
        @pl.when(z >= hop)
        def _():
            shard_copy(p, z - hop, True).wait_recv()

            @pl.when(z < nz - 1)
            def _():
                shard_copy(p, z - hop, True).start()

        @pl.when(z + hop < nz)
        def _():
            shard_copy(p, z + hop, False).wait_recv()

            @pl.when(z > 0)
            def _():
                shard_copy(p, z + hop, False).start()

    def shard_sends_done():
        for p in range(len(weight_pieces)):
            for hop in range(nz):
                @pl.when((z >= hop) & (z < nz - 1))
                def _():
                    shard_copy(p, z - hop, True).wait_send()

                @pl.when((z + hop < nz) & (z > 0))
                def _():
                    shard_copy(p, z + hop, False).wait_send()

    def block_rows(k):
        return pl.ds(pl.multiple_of(k * block, ROW_TILE), block)

    def out_copy(k):
        return pltpu.make_async_remote_copy(
            src_ref=send_rows.at[block_rows(k)],
            dst_ref=rows.at[block_rows(k)],
            send_sem=out_send.at[k],
            recv_sem=out_recv.at[k],
            device_id={"ep": lax.rem(me + k, ne)},
            device_id_type=MESH,
        )

    def pack(k, target):
        here = block_rows(k)
        first, second = pack_ref[0, here, :], pack_ref[1, here, :]
        both = first + second
        target[here, 0:model] = jnp.dot(
            both, tok_ref[...], preferred_element_type=f32
        ).astype(bf16)
        target[here, model : 2 * model] = jnp.dot(
            both, dy_ref[...], preferred_element_type=f32
        ).astype(bf16)
        target[here, 2 * model : 2 * model + LANES] = (
            jnp.dot(first, gate_wide[0], preferred_element_type=f32)
            + jnp.dot(second, gate_wide[1], preferred_element_type=f32)
        ).astype(bf16)

    def grad_copy(q, k):
        f, low, high = grad_pieces[q]
        return pltpu.make_async_remote_copy(
            src_ref=slot_grads.at[f, lax.rem(me + k, ne), :, :, low:high],
            dst_ref=peer_grads.at[f, k, :, :, low:high],
            send_sem=grad_send.at[q, k],
            recv_sem=grad_recv.at[q, k],
            device_id={"ep": lax.rem(me + k, ne)},
            device_id_type=MESH,
        )

    def sum_copy(q, dest, up):
        step = 1 if up else nz - 1
        target = from_below if up else from_above
        f, low, high = grad_pieces[q]
        return pltpu.make_async_remote_copy(
            src_ref=plane_sums.at[f, dest, :, :, low:high],
            dst_ref=target.at[f, dest, :, :, low:high],
            send_sem=sum_send.at[q, dest],
            recv_sem=sum_recv.at[q, dest, 0 if up else 1],
            device_id={"grp": lax.rem(z + step, nz)},
            device_id_type=MESH,
        )

    def pass_on(q, dest, up, first):
        f, low, high = grad_pieces[q]
        incoming = from_below if up else from_above
        if not first:
            sum_copy(q, dest, up).wait_recv()

            @pl.loop(0, experts)
            def _(e):
                plane_sums[f, dest, e, :, low:high] = (
                    plane_sums[f, dest, e, :, low:high].astype(f32)
                    + incoming[f, dest, e, :, low:high].astype(f32)
                ).astype(bf16)

        sum_copy(q, dest, up).start()

    def sum_turn(q, turn):
        lower = 2 * z < nz

        def serve(up, allowed):
            dest = nz - 1 - turn if up else turn
            edge = z == 0 if up else z == nz - 1
            short = (z < dest if up else z > dest) & allowed

            @pl.when(short & edge)
            def _():
                pass_on(q, dest, up, True)

            @pl.when(short & jnp.logical_not(edge))
            def _():
                pass_on(q, dest, up, False)

        serve(False, jnp.logical_not(lower))
        serve(True, z >= 0)
        serve(False, lower)

    def sum_level(q, level):
        @pl.when(z == level)
        def _():
            for dest in range(nz - 1, level, -1):
                pass_on(q, dest, True, level == 0)

        @pl.when(z == nz - 1 - level)
        def _():
            for dest in range(nz - 1 - level):
                pass_on(q, dest, False, level == 0)

    def ret_copy(k):
        return pltpu.make_async_remote_copy(
            src_ref=ret.at[block_rows(k)],
            dst_ref=back.at[block_rows(k)],
            send_sem=ret_send.at[k],
            recv_sem=ret_recv.at[k],
            device_id={"ep": lax.rem(me + ne - k, ne)},
            device_id_type=MESH,
        )

    def first_half(f):
        x = rows[:, 0:model]
        gate = rows[:, 2 * model : 2 * model + LANES].astype(f32)
        full = weights[f, :, :, 0 : 2 * width].reshape(model, 2 * width)
        pre = jnp.dot(x, full, preferred_element_type=f32)
        a, b = pre[:, :width], pre[:, width:]
        sig = jax.nn.sigmoid(a)
        hidden_f = (a * sig * b).astype(bf16).astype(f32)
        gated = (gate * hidden_f).astype(bf16)

        @pl.loop(0, nz)
        def _(g):
            here = pl.ds(pl.multiple_of(g * shard, shard), shard)
            dn = jnp.dot(dy_t[here, :], gated, preferred_element_type=f32).astype(bf16)
            slot_grads[f, :, g, :, 2 * width :] = dn.reshape(ne, own_rows, width)

        if f == last:
            for k in range(1, ne):
                grad_copy(last, k).start()
        return a, b, sig, hidden_f

    def second_half(f, a, b, sig, hidden_f):
        dy = rows[:, model : 2 * model]
        gate = rows[:, 2 * model : 2 * model + LANES].astype(f32)
        full = weights[f, :, :, 2 * width :].reshape(model, width)
        upstream = jnp.dot(dy, full, preferred_element_type=f32)
        gate_part = upstream * hidden_f
        if f == 0:
            gate_acc[...] = gate_part
        else:
            gate_acc[...] += gate_part
        hidden_grad = gate * upstream
        da = hidden_grad * b * sig * (1.0 + a * (1.0 - sig))
        db = hidden_grad * (a * sig)
        pre_grad = jnp.concatenate([da, db], axis=1).astype(bf16)

        @pl.loop(0, nz)
        def _(g):
            here = pl.ds(pl.multiple_of(g * shard, shard), shard)
            gu = jnp.dot(x_t[here, :], pre_grad, preferred_element_type=f32).astype(bf16)
            slot_grads[f, :, g, :, 0 : 2 * width] = gu.reshape(ne, own_rows, 2 * width)

        for k in range(1, ne):
            grad_copy(f + 1 if f == last else f, k).start()
        return pre_grad

    def row_part(f, pre_grad):
        @pl.loop(0, nz)
        def _(g):
            here = pl.ds(pl.multiple_of(g * shard, shard), shard)
            part = lax.dot_general(
                pre_grad,
                weights[f, g, :, 0 : 2 * width],
                (((1,), (1,)), ((), ())),
                preferred_element_type=f32,
            )
            if f == 0:
                row_acc[:, here] = part
            elif f < last:
                row_acc[:, here] += part
            else:
                ret[:, here] = (row_acc[:, here] + part).astype(bf16)

    def compute(f):
        row_part(f, second_half(f, *first_half(f)))

    def grads_in(q, low=1, high=ne):
        for k in range(low, high):
            grad_copy(q, k).wait_recv()

    def plane_sum(q):
        f, low, high = grad_pieces[q]

        @pl.loop(0, nz)
        def _(g):
            @pl.loop(0, own_rows // ROW_TILE)
            def _(r):
                here = pl.ds(pl.multiple_of(r * ROW_TILE, ROW_TILE), ROW_TILE)
                total = [None] * experts
                for k in range(ne):
                    if k == 0:
                        value = slot_grads[f, me, g, here, low:high].astype(f32)
                    else:
                        value = peer_grads[f, k, g, here, low:high].astype(f32)
                    for e in range(experts):
                        term = value * mask[e][k]
                        total[e] = term if total[e] is None else total[e] + term
                for e in range(experts):
                    plane_sums[f, g, e, here, low:high] = total[e].astype(bf16)

    def finish(q):
        f, low, high = grad_pieces[q]

        def add(incoming, first):
            @pl.loop(0, experts)
            def _(e):
                value = incoming[f, z, e, :, low:high].astype(f32)
                if first:
                    value = value + plane_sums[f, z, e, :, low:high].astype(f32)
                for part in range(low // width, high // width):
                    start = part * hidden_width + f * width
                    here = value[:, part * width - low : (part + 1) * width - low] / nz
                    if first:
                        wgrad_ref[e, :, start : start + width] = here
                    else:
                        wgrad_ref[e, :, start : start + width] += here

        @pl.when(z > 0)
        def _():
            sum_copy(q, z, True).wait_recv()
            add(from_below, True)

        @pl.when((z > 0) & (z < nz - 1))
        def _():
            sum_copy(q, z, False).wait_recv()
            add(from_above, False)

        @pl.when(z == 0)
        def _():
            sum_copy(q, z, False).wait_recv()
            add(from_above, True)

    start_own(0)
    for f in range(1, chunks):
        stage(f)
    if chunks > 1:
        start_own(1)

    live = [1 - failed_ref[z, s] for s in range(ne)]
    tokens_here = tok_ref.shape[0]
    square = (tokens_here, LANES)
    lane = lax.broadcasted_iota(jnp.int32, square, 1)
    hosts_row = lax.broadcasted_iota(jnp.int32, (LANES, LANES), 0)
    hosts_lane = lax.broadcasted_iota(jnp.int32, (LANES, LANES), 1)
    hosts = jnp.zeros((LANES, LANES), f32)
    replicas = jnp.zeros(square, f32)
    ordinal = jnp.zeros(square, f32)
    for s in range(ne):
        served = live[s].astype(f32)
        hosts += jnp.where(
            (hosts_row == plan_ref[s]) & (hosts_lane == s), served, 0.0
        )
        replicas += jnp.where(lane == plan_ref[s], served, 0.0)
        before = jnp.int32(0)
        for other in range(s):
            before += (plan_ref[other] == plan_ref[s]).astype(jnp.int32) * live[other]
        ordinal += jnp.where(lane == s, before.astype(f32), 0.0)
    hosts = hosts.astype(bf16)
    earlier = (
        lax.broadcasted_iota(jnp.int32, (tokens_here, tokens_here), 1)
        < lax.broadcasted_iota(jnp.int32, (tokens_here, tokens_here), 0)
    ).astype(f32).astype(bf16)

    def column(ref, k):
        return jnp.broadcast_to(ref[k : k + 1, :], (LANES, tokens_here)).T

    wanted = [
        (lane == column(route_ref, k)).astype(f32) for k in range(2)
    ]
    ranks = jnp.dot(earlier, (wanted[0] + wanted[1]).astype(bf16), preferred_element_type=f32)
    chosen = []
    for k in range(2):
        rank = jnp.sum(wanted[k] * ranks, axis=1, keepdims=True)
        n = jnp.sum(wanted[k] * replicas, axis=1, keepdims=True)
        pick = rank - n * jnp.floor((rank + 0.5) / n)
        hosting = jnp.dot(wanted[k].astype(bf16), hosts, preferred_element_type=f32)
        chosen.append(jnp.where(jnp.abs(ordinal - pick) < 0.5, hosting, 0.0))
    places = jnp.dot(earlier, (chosen[0] + chosen[1]).astype(bf16), preferred_element_type=f32)
    offset = (lax.rem(lane - me + ne, ne) * block).astype(f32)
    spot = lax.broadcasted_iota(jnp.int32, (tokens_here, count), 1)
    gate_wide = []
    for k in range(2):
        place = jnp.sum(
            jnp.where(lane < ne, chosen[k] * (places + offset), 0.0), axis=1, keepdims=True
        )
        hot = (spot == place.astype(jnp.int32)).astype(f32)
        unpack_ref[k] = hot.astype(bf16)
        pack_ref[k] = hot.T.astype(bf16)
        gate_row = jnp.broadcast_to(gate_ref[k : k + 1, :].astype(f32), (LANES, tokens_here))
        gate_wide.append(gate_row.T.astype(bf16))
    mask = []
    for e in range(experts):
        mask.append([])
        for k in range(ne):
            slot = lax.rem(me - k + ne, ne)
            hosted = (plan_ref[slot] == e).astype(jnp.int32) * (1 - failed_ref[z, slot])
            mask[e].append(hosted.astype(f32))

    @pl.loop(1, ne)
    def _(k):
        pack(k, send_rows)
        out_copy(k).start()

    pack(0, rows)

    def rows_ready():
        for k in range(1, ne):
            out_copy(k).wait_recv()

        @pl.loop(0, model // LANES)
        def _(c):
            here = pl.ds(pl.multiple_of(c * LANES, LANES), LANES)
            there = pl.ds(pl.multiple_of(model + c * LANES, LANES), LANES)
            x_t[here, :] = rows[:, here].T
            dy_t[here, :] = rows[:, there].T

    def hop_range(f, low, high):
        for hop in range(low, min(high, nz)):
            arrive(f, hop)

    duties = []

    def work():
        if duties:
            duties.pop(0)()

    def first_level(q):
        grads_in(q)
        plane_sum(q)
        sum_level(q, 0)

    def levels(q):
        duties.append(functools.partial(first_level, q))
        for level in range(1, nz - 2):
            duties.append(functools.partial(sum_level, q, level))

    def hops_between(p):
        for hop in range(1, nz):
            arrive(p, hop)
            work()

    hop_range(0, 1, nz)
    for f in range(1, last):
        start_own(f + 1)
        if f == 1:
            hop_range(1, 1, nz - 1)
            rows_ready()
            compute(0)
            hop_range(1, nz - 1, nz)
        else:
            levels(f - 2)
            hops_between(f)
        compute(f)
    start_own(last + 1)
    levels(last - 2)
    hops_between(last)
    first_level(last - 1)
    kept = first_half(last)
    hop_range(last + 1, 1, nz)
    pre_grad = second_half(last, *kept)
    for q in range(last - 1):
        sum_level(q, nz - 2)
    for level in range(1, nz - 2):
        sum_level(last - 1, level)
    row_part(last, pre_grad)
    ret[:, model : model + LANES] = jnp.broadcast_to(
        jnp.sum(gate_acc[...], axis=1, keepdims=True), (count, LANES)
    ).astype(bf16)
    first_level(last)
    for q in range(last - 1):
        finish(q)
    early = ne // 2
    grads_in(last + 1, 1, early)
    for k in range(1, early):
        ret_copy(k).start()
    grads_in(last + 1, early, ne)
    for k in range(early, ne):
        ret_copy(k).start()
    plane_sum(last + 1)
    sum_level(last - 1, nz - 2)
    for level in range(1, nz - 1):
        sum_level(last, level)
    for turn in range(nz - 1):
        sum_turn(last + 1, turn)
    for q in range(last - 1, last + 1):
        finish(q)
    back[0:block, :] = ret[0:block, :]

    for k in range(1, ne):
        ret_copy(k).wait_recv()
    first, second = unpack_ref[0], unpack_ref[1]
    both = first + second

    @pl.loop(0, nz)
    def _(g):
        here = pl.ds(pl.multiple_of(g * shard, shard), shard)
        tgrad_ref[:, here] = jnp.dot(
            both, back[:, here], preferred_element_type=f32
        ).astype(bf16)

    gates_back = back[:, model : model + LANES]
    gate_grads = jnp.where(
        lane == 0,
        jnp.dot(first, gates_back, preferred_element_type=f32),
        jnp.dot(second, gates_back, preferred_element_type=f32),
    )
    ggrad_ref[...] = gate_grads.T[0:2, :].astype(bf16)

    finish(last + 1)

    shard_sends_done()
    for k in range(1, ne):
        out_copy(k).wait_send()
        ret_copy(k).wait_send()
    for q in range(len(grad_pieces)):
        for k in range(1, ne):
            grad_copy(q, k).wait_send()
        for dest in range(nz):
            for up in (True, False):
                @pl.when(z < dest if up else z > dest)
                def _():
                    sum_copy(q, dest, up).wait_send()


def fused(tokens, out_grad, routes, gates, w_gate_up, w_down, plan, failed):
    nz = lax.axis_size("grp")
    ne = lax.axis_size("ep")
    tok_count, model = tokens.shape
    topk = routes.shape[1]
    experts = ne // 2
    capacity = tok_count * topk * 5 // (4 * ne)
    block = -(-capacity // ROW_TILE) * ROW_TILE
    count = ne * block
    shard = w_gate_up.shape[1]
    hidden_width = w_down.shape[2]
    width = LANES
    chunks = hidden_width // width
    own_rows = model // (nz * ne)
    bf16, f32 = jnp.bfloat16, jnp.float32
    vmem = pl.BlockSpec(memory_space=pltpu.VMEM)
    dma = pltpu.SemaphoreType.DMA
    tgrad, ggrad, wgrad = pl.pallas_call(
        functools.partial(fused_kernel, nz, ne, block),
        out_shape=(
            jax.ShapeDtypeStruct((tok_count, model), bf16),
            jax.ShapeDtypeStruct((topk, tok_count), bf16),
            jax.ShapeDtypeStruct((experts, own_rows, 3 * hidden_width), f32),
        ),
        in_specs=[vmem] * 6 + [pl.BlockSpec(memory_space=pltpu.SMEM)] * 2,
        out_specs=(vmem, vmem, vmem),
        scratch_shapes=[
            pltpu.VMEM((chunks, nz, shard, 3 * width), bf16),
            pltpu.VMEM((count, 2 * model + LANES), bf16),
            pltpu.VMEM((count, 2 * model + LANES), bf16),
            pltpu.VMEM((model, count), bf16),
            pltpu.VMEM((model, count), bf16),
            pltpu.VMEM((count, model), f32),
            pltpu.VMEM((count, width), f32),
            pltpu.VMEM((chunks, ne, nz, own_rows, 3 * width), bf16),
            pltpu.VMEM((chunks, ne, nz, own_rows, 3 * width), bf16),
            pltpu.VMEM((chunks, nz, experts, own_rows, 3 * width), bf16),
            pltpu.VMEM((chunks, nz, experts, own_rows, 3 * width), bf16),
            pltpu.VMEM((chunks, nz, experts, own_rows, 3 * width), bf16),
            pltpu.VMEM((count, model + LANES), bf16),
            pltpu.VMEM((count, model + LANES), bf16),
            pltpu.VMEM((topk, count, tok_count), bf16),
            pltpu.VMEM((topk, tok_count, count), bf16),
            dma((chunks + 1, nz, 2)),
            dma((chunks + 1, nz)),
            dma((ne,)),
            dma((ne,)),
            dma((chunks + 1, ne)),
            dma((chunks + 1, ne)),
            dma((chunks + 1, nz)),
            dma((chunks + 1, nz, 2)),
            dma((ne,)),
            dma((ne,)),
        ],
        compiler_params=pltpu.CompilerParams(
            collective_id=0, has_side_effects=True, vmem_limit_bytes=60 * 1024 * 1024
        ),
        cost_estimate=pl.CostEstimate(
            flops=18 * count * model * hidden_width,
            bytes_accessed=16 * 1024 * 1024,
            transcendentals=count * hidden_width,
        ),
    )(tokens, out_grad, routes.T, gates.T, w_gate_up, w_down, plan, failed)
    return (tgrad, ggrad.T, wgrad)


def local(tokens, out_grad, routes, gates, w_gate_up, w_down, plan, failed):
    groups = lax.axis_size("grp")
    slot_count = lax.axis_size("ep")
    my_group = lax.axis_index("grp")
    tok_count, model_width = tokens.shape
    topk_count = routes.shape[1]
    experts = slot_count // 2
    capacity = tok_count * topk_count * 5 // (4 * slot_count)
    route_count = tok_count * topk_count
    buffer_rows = slot_count * capacity
    in_service = 1 - lax.dynamic_index_in_dim(failed, my_group, 0, keepdims=False)
    slot_index, slot_rank = assign(routes, plan, in_service, capacity, experts)
    positions = slot_index * capacity + slot_rank
    source = (
        jnp.full((buffer_rows,), route_count, jnp.int32)
        .at[positions]
        .set(jnp.arange(route_count, dtype=jnp.int32))
    )
    token_of = source // topk_count
    zero_row = jnp.zeros((1, model_width), jnp.bfloat16)
    send_x = jnp.concatenate([tokens, zero_row], axis=0)[token_of].reshape(
        slot_count, capacity, model_width
    )
    send_dy = jnp.concatenate([out_grad, zero_row], axis=0)[token_of].reshape(
        slot_count, capacity, model_width
    )
    send_gate = jnp.concatenate([gates.reshape(route_count), jnp.zeros((1,), jnp.bfloat16)])[source]
    send_gate = send_gate.reshape(slot_count, capacity)
    recv_x, recv_dy, recv_gate = (
        lax.all_to_all(send_x, "ep", split_axis=0, concat_axis=0, tiled=True),
        lax.all_to_all(send_dy, "ep", split_axis=0, concat_axis=0, tiled=True),
        lax.all_to_all(send_gate, "ep", split_axis=0, concat_axis=0, tiled=True),
    )
    full_gu, full_dn = (
        lax.all_gather(w_gate_up, "grp", axis=1, tiled=True),
        lax.all_gather(w_down, "grp", axis=1, tiled=True),
    )
    full_gu = full_gu[0]
    full_dn = full_dn[0]
    hidden_width = full_dn.shape[1]
    flat_x = recv_x.reshape(buffer_rows, model_width)
    flat_dy = recv_dy.reshape(buffer_rows, model_width)
    flat_gate = recv_gate.reshape(buffer_rows)
    row_grads, gate_rows, grad_gu, grad_dn = expert_rows(
        flat_x, flat_dy, flat_gate, full_gu, full_dn
    )
    back_x, back_gate = (
        lax.all_to_all(
            row_grads.reshape(slot_count, capacity, model_width),
            "ep",
            split_axis=0,
            concat_axis=0,
            tiled=True,
        ),
        lax.all_to_all(
            gate_rows.reshape(slot_count, capacity), "ep", split_axis=0, concat_axis=0, tiled=True
        ),
    )
    route_rows = back_x.reshape(buffer_rows, model_width)[positions]
    token_grad = jnp.sum(
        route_rows.reshape(tok_count, topk_count, model_width).astype(jnp.float32), axis=1
    ).astype(jnp.bfloat16)
    gate_grad = back_gate.reshape(buffer_rows)[positions].reshape(tok_count, topk_count)
    columns = 3 * hidden_width
    rows_each = model_width // (groups * slot_count)
    slot_grad = jnp.concatenate([grad_gu, grad_dn], axis=1).astype(jnp.bfloat16)
    slot_grad = slot_grad.reshape(groups, slot_count, rows_each, columns)
    expert_ids = jnp.arange(experts, dtype=jnp.int32)
    mixed = lax.all_to_all(
        lax.all_to_all(slot_grad, "grp", split_axis=0, concat_axis=0, tiled=True),
        "ep",
        split_axis=1,
        concat_axis=1,
        tiled=True,
    )
    hosted_all = (
        (plan[None, None, :] == expert_ids[None, :, None]) & (failed[:, None, :] == 0)
    ).astype(jnp.bfloat16)
    per_group = jnp.einsum("ges,gsrc->gerc", hosted_all, mixed, preferred_element_type=jnp.float32)
    weight_grad = jnp.sum(per_group, axis=0) / groups
    return (token_grad, gate_grad, weight_grad)


def solution(mesh):
    nz, ne = mesh.shape["grp"], mesh.shape["ep"]

    def step(tokens, *others):
        aligned = tokens.shape[1] % (nz * ne * ROW_TILE) == 0
        return (fused if aligned else local)(tokens, *others)

    placed = (
        P(("grp", "ep"), None),
        P(("grp", "ep"), None),
        P(("grp", "ep"), None),
        P(("grp", "ep"), None),
        P("ep", "grp", None),
        P("ep", "grp", None),
        P(),
        P(),
    )
    return jax.shard_map(
        step,
        mesh=mesh,
        in_specs=placed,
        out_specs=(P(("grp", "ep"), None), P(("grp", "ep"), None), P(None, ("grp", "ep"), None)),
        check_vma=False,
    )
```
